512 devices in a mesh: lon: 32 (over x_hi, z), lat: 16 (over x_lo, y, core).
Axes of the slice: x: 4 (x_hi: 2, x_lo: 2; x = x_hi * 2 + x_lo), y: 4, z: 16, core: 2. Of those that a mesh axis runs over, the one named last changes fastest.
Arguments:
- fields: float32 [4, 10, 256, 4096], P(None, None, 'lat', 'lon'), may hold values from -4 to 4
- sea_mask: int32 [10, 256, 4096], P(None, 'lat', 'lon'), may hold values from 0 to 1, as said below
- bottom_level: int32 [256, 4096], P('lat', 'lon'), may hold values from 0 to 10, as said below
- coriolis: float32 [256, 4096], P('lat', 'lon'), may hold values from -1 to 1
Outputs:
- new_fields: float32 [4, 10, 256, 4096], P(None, None, 'lat', 'lon')
The draws below stay inside these ranges and needn't reach their ends.
Inputs may be any that keep to these rules, and one draw needn't show every extreme that they name: sea_mask[k, y, x] is 1 exactly where k < bottom_level[y, x]. `bottom_level`: 0 marks a land column.
All inputs are finite; a program needn't handle non-finite values.
Results may differ from the reference program's by a relative error of at most 0.0003.
Values sent between devices are 32-bit elements; how exact they have to be, the bound alone decides.
No kernel may reach another device: no remote copies, remote signals or barrier semaphores. Data moves between devices by JAX's collectives and lax.ppermute only.
A program may use at most 64 MiB of HBM per device.

```python
import jax
import jax.numpy as jnp
from jax import lax

LEVELS = 10
STEPS = 4
NX = 4096
NY = 256


def column_depth(key):
    land = jax.random.randint(jax.random.fold_in(key, 11), (NY, NX), 0, 5) == 0
    depth = jax.random.randint(jax.random.fold_in(key, 12), (NY, NX), 1, LEVELS + 1)
    return jnp.where(land, 0, depth).astype(jnp.int32)


def draw_sea_mask(key, part):
    depth = column_depth(key)
    level_ids = lax.broadcasted_iota(jnp.int32, (LEVELS, NY, NX), 0)
    return (level_ids < depth[None]).astype(jnp.int32)


def draw_bottom_level(key, part):
    return column_depth(key)


def block_levels(rng, extent, pieces, smallest, top_value):
    level, own = 1.0, jax.random.fold_in(rng, 6)
    for position, shards_of in pieces:
        steps = jnp.exp(jax.random.uniform(jax.random.fold_in(own, position), (shards_of,), jnp.float32, smallest / len(pieces), top_value / len(pieces)))
        level = level * jnp.repeat(steps, extent[position] // shards_of).reshape([-1 if axis == position else 1 for axis in range(len(extent))])
    return level


def scatter_about(stream_key, extent, width, most, cuts=(), kind=jnp.bfloat16):
    loudness = block_levels(stream_key, extent, cuts, -0.22, 0.18) if cuts else 1.0
    drawn = jax.random.normal(stream_key, extent, jnp.float32) * width * loudness
    return jnp.minimum(jnp.maximum(drawn, -most), most).astype(kind)


def setup_inputs(seed: int = 0) -> dict:
    key_of = jax.random.split(jax.random.key(seed), 5)
    fields = scatter_about(key_of[0], (4, LEVELS, NY, NX), 1.0, 4.0, ((2, 16), (3, 32)), jnp.float32)
    sea_mask = draw_sea_mask(jax.random.fold_in(key_of[4], 71), 0)
    bottom_level = draw_bottom_level(jax.random.fold_in(key_of[4], 71), 0)
    coriolis = jnp.clip(jax.random.uniform(key_of[3], (NY, NX), jnp.float32, -1.0, 1.0) * block_levels(key_of[3], (NY, NX), ((0, 16), (1, 32)), -0.4, 0.0), -1.0, 1.0)
    return {"fields": fields, "sea_mask": sea_mask, "bottom_level": bottom_level, "coriolis": coriolis}


STEP_DT = 0.1
KAPPA = 0.2
DRAG_RATE = 0.5
GRAVITY = 0.1
ALPHA_T = 0.2
BETA_S = 0.15


def laplace(field, wetness):
    height = field.shape[-2]
    breadth = field.shape[-1]
    inside = field[..., 1:-1, 1:-1]
    wet_in = wetness[..., 1:-1, 1:-1]
    summed = jnp.zeros_like(inside)
    for shift_y, shift_x in ((0, 1), (2, 1), (1, 0), (1, 2)):
        beside = field[..., shift_y:shift_y + height - 2, shift_x:shift_x + breadth - 2]
        wet_beside = wetness[..., shift_y:shift_y + height - 2, shift_x:shift_x + breadth - 2]
        summed = summed + wet_in * wet_beside * (beside - inside)
    return summed


def advance(padded, wet_pad, pressure, coriolis, drag_on):
    center = padded[..., 2:-2, 2:-2]
    slope_east = 0.5 * (padded[..., 2:-2, 4:] - padded[..., 2:-2, :-4])
    slope_north = 0.5 * (padded[..., 4:, 2:-2] - padded[..., :-4, 2:-2])
    zonal_flow = center[2]
    merid_flow = center[3]
    carried = -(zonal_flow * slope_east + merid_flow * slope_north)
    first_pass = laplace(padded, wet_pad)
    smooth = laplace(first_pass, wet_pad[..., 1:-1, 1:-1])
    press_east = 0.5 * (pressure[..., 2:-2, 4:] - pressure[..., 2:-2, :-4])
    press_north = 0.5 * (pressure[..., 4:, 2:-2] - pressure[..., :-4, 2:-2])
    force_east = coriolis * merid_flow - press_east - DRAG_RATE * drag_on * zonal_flow
    force_north = -coriolis * zonal_flow - press_north - DRAG_RATE * drag_on * merid_flow
    nothing = jnp.zeros_like(force_east)
    forcing = jnp.stack([nothing, nothing, force_east, force_north])
    tendency = carried - KAPPA * smooth + forcing
    return wet_pad[..., 2:-2, 2:-2] * (center + STEP_DT * tendency)


def extend_global(field, signs):
    folded = field[..., -1:-3:-1, ::-1] * signs
    south = jnp.zeros_like(field[..., :2, :])
    tall = jnp.concatenate([south, field, folded], axis=-2)
    return jnp.concatenate([tall[..., -2:], tall, tall[..., :2]], axis=-1)


def reference(fields, sea_mask, bottom_level, coriolis):
    wetness = sea_mask.astype(jnp.float32)
    signs = jnp.array([1.0, 1.0, -1.0, -1.0], jnp.float32).reshape(4, 1, 1)
    level_ids = jnp.arange(LEVELS, dtype=jnp.int32)
    state = fields
    for step_index in range(STEPS):
        def per_level(above, inputs):
            layer, wet_layer, level = inputs
            padded = extend_global(layer, signs)
            wet_pad = extend_global(wet_layer, 1.0)
            density = BETA_S * padded[1] - ALPHA_T * padded[0]
            pressure = above + GRAVITY * density
            drag_on = (bottom_level - 1 == level).astype(jnp.float32)
            return pressure, advance(padded, wet_pad, pressure, coriolis, drag_on)

        start = jnp.zeros((NY + 4, NX + 4), jnp.float32)
        final_pressure, layers = lax.scan(per_level, start, (jnp.moveaxis(state, 1, 0), wetness, level_ids))
        state = jnp.moveaxis(layers, 0, 1)
    return state
```

```python
import functools

import jax
import jax.numpy as jnp
from jax import lax
from jax.experimental import pallas as pl
from jax.experimental.pallas import tpu as pltpu
from jax.sharding import PartitionSpec as P

STEPS = 4
STEP_DT = 0.1
KAPPA = 0.2
DRAG_RATE = 0.5
GRAVITY = 0.1
ALPHA_T = 0.2
BETA_S = 0.15

COMPS = 4
LEVELS = 10
PAIRS = LEVELS // 2
SLABS = LEVELS + PAIRS
PLANES = COMPS * LEVELS + 2
ROWS = 16
HALO = 8
EXT = ROWS + 2 * HALO
PITCH = EXT + 16
LANES = 128
GROUPS = 3


def lane_ids(rows):
    return lax.broadcasted_iota(jnp.int32, (rows, LANES), 1)


def turned(by):
    if by % LANES == 0:
        return lambda value: value
    return lambda value: pltpu.roll(value, by % LANES, 1)


def beside(value):
    return turned(-1)(value + turned(2)(value))


def sloped(value):
    return turned(-2)(value) - turned(2)(value)


def beside_and_sloped(value):
    two_west = turned(2)(value)
    return turned(-1)(value + two_west), turned(-2)(value) - two_west


def pack_lat_kernel(lat_ref, fields_ref, bottom_ref, coriolis_ref, first_ref, second_ref, *, lat_count):
    lat = lat_ref[0]
    even = lat % 2 == 0
    first_row = pl.multiple_of(jnp.where(even, HALO, 0), HALO)
    second_row = pl.multiple_of(jnp.where(even, 0, HALO), HALO)

    def copied(row, out_ref):
        for comp in range(COMPS):
            for level in range(LEVELS):
                out_ref[comp * LEVELS + level] = fields_ref[comp, level, pl.ds(row, HALO), :]
        out_ref[PLANES - 2] = bottom_ref[pl.ds(row, HALO), :].astype(jnp.float32)
        out_ref[PLANES - 1] = coriolis_ref[pl.ds(row, HALO), :]

    copied(first_row, first_ref)
    copied(second_row, second_ref)

    @pl.when(lat == lat_count - 1)
    def _():
        lanes = LANES - 1 - lane_ids(HALO)
        rows = HALO - 1 - lax.broadcasted_iota(jnp.int32, (HALO, LANES), 0)
        for plane in range(PLANES):
            value = second_ref[plane]
            value = jnp.take_along_axis(value, lanes, axis=1)
            value = jnp.take_along_axis(value, rows, axis=0)
            if 2 * LEVELS <= plane < 4 * LEVELS:
                value = -value
            second_ref[plane] = value


def extended(plane, own, first, second, even):
    one, two = first[plane], second[plane]
    south = jnp.where(even, two, one)
    north = jnp.where(even, one, two)
    return south, own, north


def pack_lon_kernel(lat_ref, fields_ref, bottom_ref, coriolis_ref, first_ref, second_ref, west_ref, east_ref):
    even = lat_ref[0] % 2 == 0
    lanes = lane_ids(EXT)

    def ext(plane, own):
        return jnp.concatenate(extended(plane, own, first_ref, second_ref, even), axis=0)

    def pair(index):
        if index < COMPS * PAIRS:
            comp, level = divmod(index, PAIRS)
            return (
                ext(comp * LEVELS + level, fields_ref[comp, level]),
                ext(comp * LEVELS + level + PAIRS, fields_ref[comp, level + PAIRS]),
            )
        if index == COMPS * PAIRS:
            value = ext(PLANES - 2, bottom_ref[...].astype(jnp.float32))
        else:
            value = ext(PLANES - 1, coriolis_ref[...])
        return value, value

    for group in range(GROUPS):
        west = jnp.zeros((EXT, LANES), jnp.float32)
        east = jnp.zeros((EXT, LANES), jnp.float32)
        for slot in range(8):
            index = 8 * group + slot
            if index >= COMPS * PAIRS + 2:
                continue
            for half, value in enumerate(pair(index)):
                at = 64 * half + 8 * slot
                here = (lanes >= at) & (lanes < at + 8)
                west = jnp.where(here, turned(at)(value), west)
                east = jnp.where(here, turned(at + HALO)(value), east)
        west_ref[group] = west
        east_ref[group] = east


def steps_kernel(
    lat_ref, fields_ref, bottom_ref, coriolis_ref, first_ref, second_ref, from_west_ref, from_east_ref,
    out_ref, raw, ping, pong, wet, count, lap, flat,
):
    even = lat_ref[0] % 2 == 0
    lanes = lane_ids(EXT)
    upper = lanes >= 64
    place = lanes % 64

    def at(comp, slab):
        return (comp * SLABS + slab) * PITCH + 8

    def put(ref, start, value):
        ref[pl.ds(start, value.shape[0]), :] = value

    def ext(plane, own):
        return jnp.concatenate(extended(plane, own, first_ref, second_ref, even), axis=0)

    def strip(index, low, high):
        group, slot = divmod(index, 8)
        value = jnp.where(upper, turned(64 + 8)(high), turned(8)(low))
        value = jnp.where((place >= 24) & (place < 40), jnp.where(upper, turned(64 + 40)(high), turned(40)(low)), value)
        value = jnp.where(place < 8, turned(-8 * slot)(from_west_ref[group]), value)
        value = jnp.where((place >= 40) & (place < 48), turned(40 - 8 * slot)(from_east_ref[group]), value)
        return value

    bottom = ext(PLANES - 2, bottom_ref[...].astype(jnp.float32))
    bottom_strip = strip(COMPS * PAIRS, bottom, bottom)
    twist = ext(PLANES - 1, coriolis_ref[...])
    twist_strip = strip(COMPS * PAIRS + 1, twist, twist)
    for slot, value in enumerate((bottom, bottom_strip, STEP_DT * twist, STEP_DT * twist_strip)):
        put(flat, slot * PITCH + 8, value)
    high_level = jnp.where(upper, float(PAIRS), 0.0)
    for slab in range(SLABS):
        if slab < LEVELS:
            value = jnp.where(bottom > slab, 1.0, 0.0)
        else:
            value = jnp.where(bottom_strip > (slab - LEVELS) + high_level, 1.0, 0.0)
        put(wet, slab * PITCH + 8, value)
    for slab in range(SLABS):
        start = slab * PITCH + 8
        value = wet[pl.ds(start, EXT), :]
        around = (wet[pl.ds(start - 1, EXT), :] + wet[pl.ds(start + 1, EXT), :]) + beside(value)
        put(count, start, around)

    for comp in range(COMPS):
        for level in range(PAIRS):
            low = ext(comp * LEVELS + level, fields_ref[comp, level])
            high = ext(comp * LEVELS + level + PAIRS, fields_ref[comp, level + PAIRS])
            both = strip(comp * PAIRS + level, low, high)
            for slab, value in ((level, low), (level + PAIRS, high), (LEVELS + level, both)):
                put(raw, at(comp, slab), value)
                put(ping, at(comp, slab), value * wet[pl.ds(slab * PITCH + 8, EXT), :])

    def advance(step, slabs, source, target, a_window, b_window, finish=None):
        a_row, a_rows = a_window
        b_row, b_rows = b_window
        aligned = a_window == b_window
        is_strip = slabs[0] >= LEVELS
        slope_of = raw if step == 0 else source
        bottom_at = (1 if is_strip else 0) * PITCH + 8
        twist_at = (3 if is_strip else 2) * PITCH + 8
        b_lanes = lane_ids(b_rows)

        def body(slab, carry):
            press_east, press_north = carry
            mask_at = pl.multiple_of(slab * PITCH, 8) + 8
            w_a = wet[pl.ds(mask_at + a_row, a_rows), :]
            n_a = count[pl.ds(mask_at + a_row, a_rows), :]
            if aligned:
                w_b, n_b = w_a, n_a
            else:
                w_b = wet[pl.ds(mask_at + b_row, b_rows), :]
                n_b = count[pl.ds(mask_at + b_row, b_rows), :]
            east_slope, centre = [], []
            for comp in range(COMPS):
                start = pl.multiple_of((comp * SLABS + slab) * PITCH, 8) + 8
                value = source[pl.ds(start + a_row, a_rows), :]
                north = source[pl.ds(start + a_row + 1, a_rows), :]
                south = source[pl.ds(start + a_row - 1, a_rows), :]
                if step > 0 and aligned:
                    lateral, slope = beside_and_sloped(value)
                else:
                    lateral = beside(value)
                put(lap, comp * PITCH + 8 + a_row, w_a * ((north + south) + lateral - n_a * value))
                if step == 0:
                    slope = sloped(raw[pl.ds(start + b_row, b_rows), :])
                elif not aligned:
                    value = source[pl.ds(start + b_row, b_rows), :]
                    slope = sloped(value)
                east_slope.append(slope)
                centre.append(value)
            north_slope = []
            for comp in range(COMPS):
                start = pl.multiple_of((comp * SLABS + slab) * PITCH, 8) + 8
                north_slope.append(slope_of[pl.ds(start + b_row + 2, b_rows), :] - slope_of[pl.ds(start + b_row - 2, b_rows), :])
            scale = 0.5 * STEP_DT * GRAVITY
            press_east = press_east + (scale * BETA_S) * east_slope[1] - (scale * ALPHA_T) * east_slope[0]
            press_north = press_north + (scale * BETA_S) * north_slope[1] - (scale * ALPHA_T) * north_slope[0]
            twist_b = flat[pl.ds(twist_at + b_row, b_rows), :]
            bottom_b = flat[pl.ds(bottom_at + b_row, b_rows), :]
            if is_strip:
                level = (slab - LEVELS).astype(jnp.float32) + jnp.where(b_lanes >= 64, float(PAIRS), 0.0)
            else:
                level = slab.astype(jnp.float32)
            keep = 1.0 - jnp.where(bottom_b - 1.0 == level, STEP_DT * DRAG_RATE, 0.0)
            zonal = (-0.5 * STEP_DT) * centre[2]
            merid = (-0.5 * STEP_DT) * centre[3]
            for comp in range(COMPS):
                start = pl.multiple_of((comp * SLABS + slab) * PITCH, 8) + 8
                lap_at = comp * PITCH + 8 + b_row
                value = lap[pl.ds(lap_at, b_rows), :]
                around = lap[pl.ds(lap_at + 1, b_rows), :] + lap[pl.ds(lap_at - 1, b_rows), :]
                smooth = around + beside(value) - n_b * value
                new = zonal * east_slope[comp] + merid * north_slope[comp] - (STEP_DT * KAPPA) * smooth
                if comp < 2:
                    new = new + centre[comp]
                elif comp == 2:
                    new = new + (keep * centre[2] + twist_b * centre[3] - press_east)
                else:
                    new = new + (keep * centre[3] - twist_b * centre[2] - press_north)
                new = w_b * new
                if finish is None:
                    put(target, start + b_row, new)
                else:
                    finish(comp, slab, new)
            return press_east, press_north

        if is_strip:
            total = None
            for slab in slabs:
                salt = slope_of[pl.ds(at(1, slab), EXT), :]
                heat = slope_of[pl.ds(at(0, slab), EXT), :]
                term = BETA_S * salt - ALPHA_T * heat
                total = term if total is None else total + term
            base = (0.5 * STEP_DT * GRAVITY) * jnp.where(upper, turned(64)(total), 0.0)
            base_at = 4 * PITCH + 8
            put(flat, base_at, base)
            middle = flat[pl.ds(base_at + b_row, b_rows), :]
            carry = (
                sloped(middle),
                flat[pl.ds(base_at + b_row + 2, b_rows), :] - flat[pl.ds(base_at + b_row - 2, b_rows), :],
            )
        else:
            carry = (jnp.zeros((b_rows, LANES), jnp.float32),) * 2
        lax.fori_loop(slabs[0], slabs[-1] + 1, body, carry)

    own_lanes = lane_ids(ROWS)

    def finish(comp, slab, new):
        high = slab >= PAIRS
        start = pl.multiple_of((comp * SLABS + LEVELS + slab % PAIRS) * PITCH, 8) + 8 + HALO
        edge = ping[pl.ds(start, ROWS), :]
        edge = jnp.where(high, turned(64)(edge), edge)
        new = jnp.where(own_lanes < 8, turned(-8)(edge), new)
        new = jnp.where(own_lanes >= 120, turned(120 - 32)(edge), new)
        out_ref[comp, slab] = new

    windows = (
        ((0, EXT), (0, EXT)),
        ((0, EXT), (0, EXT)),
        ((4, EXT - 8), (4, EXT - 8)),
        ((4, EXT - 8), (HALO, ROWS)),
    )
    for slabs in (range(LEVELS, SLABS), range(LEVELS)):
        source, target = ping, pong
        for step in range(STEPS):
            last = step == STEPS - 1 and slabs[0] == 0
            advance(step, slabs, source, target, *windows[step], finish if last else None)
            source, target = target, source


def vmem(count):
    return [pl.BlockSpec(memory_space=pltpu.VMEM)] * count


def call(kernel, out_shape, scratch, flops, moved, *operands):
    lat, *arrays = operands
    return pl.pallas_call(
        kernel,
        out_shape=out_shape,
        in_specs=[pl.BlockSpec(memory_space=pltpu.SMEM)] + vmem(len(arrays)),
        out_specs=jax.tree.map(lambda _: pl.BlockSpec(memory_space=pltpu.VMEM), out_shape),
        scratch_shapes=scratch,
        compiler_params=pltpu.CompilerParams(vmem_limit_bytes=32 << 20),
        cost_estimate=pl.CostEstimate(flops=flops, bytes_accessed=moved, transcendentals=0),
    )(lat, *arrays)


def local(fields, sea_mask, bottom_level, coriolis):
    del sea_mask
    lat_count, lon_count = lax.axis_size("lat"), lax.axis_size("lon")
    lat = lax.axis_index("lat").astype(jnp.int32).reshape(1)
    axes = ("lon", "lat")
    flat = lambda lon, row: (lon % lon_count) * lat_count + row
    f32 = lambda *shape: jax.ShapeDtypeStruct(shape, jnp.float32)

    everywhere = [(lon, row) for lon in range(lon_count) for row in range(lat_count)]
    first_pairs = [(flat(lon, row), flat(lon, row ^ 1)) for lon, row in everywhere]
    second_pairs = []
    for lon, row in everywhere:
        if row == lat_count - 1:
            second_pairs.append((flat(lon, row), flat(lon_count - 1 - lon, row)))
        elif row > 0:
            second_pairs.append((flat(lon, row), flat(lon, ((row + 1) ^ 1) - 1)))
    east_pairs = [(flat(lon, row), flat(lon + 1, row)) for lon, row in everywhere]
    west_pairs = [(flat(lon, row), flat(lon - 1, row)) for lon, row in everywhere]

    lat_message = f32(PLANES, HALO, LANES)
    to_first, to_second = call(
        functools.partial(pack_lat_kernel, lat_count=lat_count), (lat_message,) * 2, (), 10**5, 10**6,
        lat, fields, bottom_level, coriolis,
    )
    second = lax.ppermute(to_second, axes, second_pairs)
    first = lax.ppermute(to_first, axes, first_pairs)
    lon_message = f32(GROUPS, EXT, LANES)
    to_west, to_east = call(
        pack_lon_kernel, (lon_message,) * 2, (), 10**5, 10**6,
        lat, fields, bottom_level, coriolis, first, second,
    )
    from_west = lax.ppermute(to_east, axes, east_pairs)
    from_east = lax.ppermute(to_west, axes, west_pairs)
    state = pltpu.VMEM((COMPS * SLABS * PITCH, LANES), jnp.float32)
    masks = pltpu.VMEM((SLABS * PITCH, LANES), jnp.float32)
    scratch = (state, state, state, masks, masks) + (
        pltpu.VMEM((COMPS * PITCH, LANES), jnp.float32), pltpu.VMEM((5 * PITCH, LANES), jnp.float32),
    )
    return call(
        steps_kernel, f32(COMPS, LEVELS, ROWS, LANES), scratch, 2 * 10**7, 10**6,
        lat, fields, bottom_level, coriolis, first, second, from_west, from_east,
    )


def solution(mesh):
    in_specs = (P(None, None, "lat", "lon"), P(None, "lat", "lon"), P("lat", "lon"), P("lat", "lon"))
    out_specs = P(None, None, "lat", "lon")
    return jax.shard_map(local, mesh=mesh, in_specs=in_specs, out_specs=out_specs, check_vma=False)
```

```python
import functools

import jax
import jax.numpy as jnp
from jax import lax
from jax.experimental import pallas as pl
from jax.experimental.pallas import tpu as pltpu
from jax.sharding import PartitionSpec as P

STEPS = 4
STEP_DT = 0.1
KAPPA = 0.2
DRAG_RATE = 0.5
GRAVITY = 0.1
ALPHA_T = 0.2
BETA_S = 0.15

COMPS = 4
LEVELS = 10
PAIRS = LEVELS // 2
PLANES = COMPS * LEVELS + 2
ROWS = 16
HALO = 8
EXT = ROWS + 2 * HALO
PITCH = EXT + 16
LANES = 128
BATCH = 5
LAG = 1
LIMIT = 56
GROUPS = 3


def lane_ids(rows):
    return lax.broadcasted_iota(jnp.int32, (rows, LANES), 1)


def turned(by):
    if by % LANES == 0:
        return lambda value: value
    return lambda value: pltpu.roll(value, by % LANES, 1)


def beside(value):
    return turned(-1)(value) + turned(1)(value)


def sloped(value):
    return turned(-2)(value) - turned(2)(value)


def in_two(value):
    high = value.astype(jnp.bfloat16)
    low = (value - high.astype(jnp.float32)).astype(jnp.bfloat16)
    return jnp.concatenate([high, low], axis=1)


def neighbours():
    source = lax.broadcasted_iota(jnp.int32, (2 * LANES, 2 * LANES), 0) % LANES
    target = lax.broadcasted_iota(jnp.int32, (2 * LANES, 2 * LANES), 1)
    east = (source - target) % LANES
    sums = jnp.where((east == 1) | (east == LANES - 1), 1.0, 0.0)
    slopes = jnp.where(east == 2, 1.0, jnp.where(east == LANES - 2, -1.0, 0.0))
    return jnp.where(target < LANES, sums, slopes).astype(jnp.bfloat16)


def pairs_of(plane_of):
    for index in range(COMPS * PAIRS + 2):
        comp, level = divmod(index, PAIRS)
        if comp < COMPS:
            low = plane_of(comp * LEVELS + level)
            yield index, low, plane_of(comp * LEVELS + level + PAIRS)
        else:
            value = plane_of(COMPS * LEVELS + index - COMPS * PAIRS)
            yield index, value, value


def plane_reader(fields_ref, flat_ref):
    def read(plane, start, rows):
        if plane >= COMPS * LEVELS:
            return flat_ref[plane - COMPS * LEVELS, pl.ds(start, rows), :]
        return fields_ref[plane // LEVELS, plane % LEVELS, pl.ds(start, rows), :]

    return read


def folded(value, lanes):
    rows = HALO - 1 - lax.broadcasted_iota(jnp.int32, (HALO, LANES), 0)
    return jnp.take_along_axis(jnp.take_along_axis(value, lanes, axis=1), rows, axis=0)


def pack_second_kernel(
    lat_ref, fields_any, bottom_any, coriolis_any, second_ref, rows_ref, bottom_ref, coriolis_ref, semaphores, *, lat_count
):
    lat = lat_ref[0]
    row = pl.multiple_of(jnp.where(lat % 2 == 0, 0, HALO), HALO)
    here = pl.ds(row, HALO)
    copies = [
        pltpu.make_async_copy(source, target, semaphores.at[index])
        for index, (source, target) in enumerate((
            (fields_any.at[:, :, here, :], rows_ref),
            (bottom_any.at[here, :], bottom_ref),
            (coriolis_any.at[here, :], coriolis_ref),
        ))
    ]
    for copy in copies:
        copy.start()
    for copy in copies:
        copy.wait()

    def read(plane):
        if plane < COMPS * LEVELS:
            return rows_ref[plane // LEVELS, plane % LEVELS]
        return bottom_ref[...].astype(jnp.float32) if plane == PLANES - 2 else coriolis_ref[...]

    second_ref[PLANES] = jnp.zeros((HALO, LANES), jnp.float32)

    @pl.when(lat < lat_count - 1)
    def _():
        for plane in range(PLANES):
            second_ref[plane] = read(plane)

    @pl.when(lat == lat_count - 1)
    def _():
        back = LANES - 1 - lane_ids(HALO)
        for plane in range(PLANES):
            value = folded(read(plane), back)
            second_ref[plane] = -value if 2 * LEVELS <= plane < 4 * LEVELS else value


def pack_first_kernel(lat_ref, fields_ref, flat_ref, first_ref):
    read = plane_reader(fields_ref, flat_ref)
    row = pl.multiple_of(jnp.where(lat_ref[0] % 2 == 0, HALO, 0), HALO)
    for plane in range(PLANES):
        first_ref[plane] = read(plane, row, HALO)


def pack_sides_kernel(lat_ref, lon_ref, fields_ref, flat_ref, second_ref, first_ref, to_second_ref, to_first_ref):
    read, joined = plane_reader(fields_ref, flat_ref), joiner(lat_ref)
    lanes = lane_ids(EXT)
    west = [jnp.zeros((EXT, LANES), jnp.float32) for _ in range(GROUPS)]
    east = list(west)
    for index, low, high in pairs_of(lambda plane: joined(first_ref[plane], read(plane, 0, ROWS), second_ref[plane])):
        group, slot = divmod(index, 8)
        for at, value in ((8 * slot, low), (8 * slot + 64, high)):
            here = (lanes >= at) & (lanes < at + 8)
            west[group] = jnp.where(here, turned(at)(value), west[group])
            east[group] = jnp.where(here, turned(at + HALO)(value), east[group])
    for group in range(GROUPS):
        even = lon_ref[0] % 2 == 0
        to_second_ref[group] = jnp.where(even, west[group], east[group])
        to_first_ref[group] = jnp.where(even, east[group], west[group])


def joiner(lat_ref):
    even = lat_ref[0] % 2 == 0

    def joined(one, own, two):
        return jnp.concatenate([jnp.where(even, two, one), own, jnp.where(even, one, two)], axis=0)

    return joined


def evolve(scratch, slabs, strips, plain_of, bottom, twist, finish):
    raw, state, lap, east_diff, north_diff, wet, count, flat, press, matrix = scratch

    def at(slab, comp=0):
        return (comp * slabs + slab) * PITCH + 8

    def get(ref, start, rows):
        return ref[pl.ds(start, rows), :]

    def put(ref, start, value):
        ref[pl.ds(start, value.shape[0]), :] = value

    matrix[...] = neighbours()
    if strips:
        bottom = bottom - jnp.where(lane_ids(EXT) >= 64, float(PAIRS), 0.0)
    put(flat, 8, bottom)
    put(flat, PITCH + 8, STEP_DT * twist)
    for slab in range(slabs):
        value = jnp.where(bottom > float(slab), 1.0, 0.0)
        put(wet, at(slab), value)
        around = (get(wet, at(slab) - 1, EXT) + get(wet, at(slab) + 1, EXT)) + beside(value)
        put(count, at(slab), around)
        for comp in range(COMPS):
            plain = plain_of(comp, slab)
            put(raw, at(slab, comp), plain)
            put(state, at(slab, comp), plain * value)

    a_windows = ((0, EXT), (0, EXT), (4, EXT - 8), (0, EXT))
    b_windows = ((0, EXT), (0, EXT), (4, EXT - 8), (HALO, ROWS))

    def before(step, batch):
        a_row, a_rows = a_windows[step]
        b_row, b_rows = b_windows[step]
        slope_of = raw if step == 0 else state
        fields = [(slab, comp) for slab in batch for comp in range(COMPS)]

        def lateral(ref):
            values = [in_two(get(ref, at(*field) + a_row, a_rows)) for field in fields]
            return jnp.dot(jnp.concatenate(values, axis=0), matrix[...], preferred_element_type=jnp.float32)

        both = lateral(state)
        slopes = lateral(raw) if step == 0 else both
        for index, (slab, comp) in enumerate(fields):
            w = get(wet, at(slab) + a_row, a_rows)
            n = get(count, at(slab) + a_row, a_rows)
            start = at(slab, comp)
            value = get(state, start + a_row, a_rows)
            along = get(state, start + a_row + 1, a_rows) + get(state, start + a_row - 1, a_rows)
            sums = both[index * a_rows : (index + 1) * a_rows, :LANES]
            put(lap, start + a_row, w * (along + sums - n * value))
            first = index * a_rows + b_row - a_row
            put(east_diff, start + b_row, slopes[first : first + b_rows, LANES:])
            put(north_diff, start + b_row, get(slope_of, start + b_row + 2, b_rows) - get(slope_of, start + b_row - 2, b_rows))

    scale = 0.5 * STEP_DT * GRAVITY

    def heavier(ref, slab, row, rows):
        return (scale * BETA_S) * get(ref, at(slab, 1) + row, rows) - (scale * ALPHA_T) * get(ref, at(slab, 0) + row, rows)

    def base(step):
        row, rows = b_windows[step]
        for slot, ref in enumerate((east_diff, north_diff)):
            total = None
            for slab in range(slabs):
                term = heavier(ref, slab, row, rows)
                total = term if total is None else total + term
            put(press, slot * PITCH + 8 + row, jnp.where(lane_ids(rows) >= 64, turned(64)(total), 0.0))

    def after(step, slab):
        row, rows = b_windows[step]
        w = get(wet, at(slab) + row, rows)
        n = get(count, at(slab) + row, rows)
        slopes = []
        for slot, ref in enumerate((east_diff, north_diff)):
            slope = heavier(ref, slab, row, rows)
            press_at = slot * PITCH + 8 + row
            if slab > 0 or strips:
                slope = slope + get(press, press_at, rows)
            put(press, press_at, slope)
            slopes.append(slope)
        twist_b = get(flat, PITCH + 8 + row, rows)
        bottom_b = get(flat, 8 + row, rows)
        keep = jnp.where(bottom_b == float(slab + 1), 1.0 - STEP_DT * DRAG_RATE, 1.0)
        old_zonal = get(state, at(slab, 2) + row, rows)
        old_merid = get(state, at(slab, 3) + row, rows)
        zonal = (-0.5 * STEP_DT) * old_zonal
        merid = (-0.5 * STEP_DT) * old_merid
        for comp in range(COMPS):
            start = at(slab, comp) + row
            value = get(lap, start, rows)
            along = get(lap, start + 1, rows) + get(lap, start - 1, rows)
            smooth = along + beside(value) - n * value
            new = zonal * get(east_diff, start, rows) + merid * get(north_diff, start, rows) - (STEP_DT * KAPPA) * smooth
            if comp < 2:
                new = new + get(state, start, rows)
            elif comp == 2:
                new = new + (keep * old_zonal + twist_b * old_merid - slopes[0])
            else:
                new = new + (keep * old_merid - twist_b * old_zonal - slopes[1])
            new = w * new
            if step < STEPS - 1:
                put(state, start, new)
            else:
                finish(comp, slab, new)

    batches = [tuple(range(first, min(first + BATCH, slabs))) for first in range(0, slabs, BATCH)]
    for batch in batches:
        before(0, batch)
    for step in range(STEPS):
        if strips:
            base(step)
        waiting = []
        for batch in batches:
            for slab in batch:
                after(step, slab)
            waiting.append(batch)
            if step < STEPS - 1 and len(waiting) > LAG:
                before(step + 1, waiting.pop(0))
        if step < STEPS - 1:
            for batch in waiting:
                before(step + 1, batch)


def block_kernel(lat_ref, fields_ref, flat_ref, second_ref, first_ref, out_ref, *scratch):
    read, joined = plane_reader(fields_ref, flat_ref), joiner(lat_ref)

    def ext(plane):
        return joined(first_ref[plane], read(plane, 0, ROWS), second_ref[plane])

    def finish(comp, slab, new):
        out_ref[comp, slab] = new

    evolve(
        scratch, LEVELS, False, lambda comp, slab: ext(comp * LEVELS + slab), ext(PLANES - 2), ext(PLANES - 1), finish
    )


def strips_kernel(
    lat_ref, lon_ref, fields_ref, flat_ref, second_ref, first_ref, second_side_ref, first_side_ref, block_ref, out_ref, *scratch
):
    read, joined = plane_reader(fields_ref, flat_ref), joiner(lat_ref)
    lanes = lane_ids(EXT)
    upper = lanes >= 64
    place = lanes % 64

    def ext(plane):
        return joined(first_ref[plane], read(plane, 0, ROWS), second_ref[plane])

    even = lon_ref[0] % 2 == 0
    from_west = [jnp.where(even, second_side_ref[group], first_side_ref[group]) for group in range(GROUPS)]
    from_east = [jnp.where(even, first_side_ref[group], second_side_ref[group]) for group in range(GROUPS)]

    def strip(index, low, high):
        group, slot = divmod(index, 8)
        value = jnp.where(upper, turned(64 + 8)(high), turned(8)(low))
        value = jnp.where((place >= 24) & (place < 40), jnp.where(upper, turned(64 + 40)(high), turned(40)(low)), value)
        value = jnp.where(place < 8, turned(-8 * slot)(from_west[group]), value)
        value = jnp.where((place >= 40) & (place < 48), turned(40 - 8 * slot)(from_east[group]), value)
        return value

    def plain_of(comp, slab):
        return strip(comp * PAIRS + slab, ext(comp * LEVELS + slab), ext(comp * LEVELS + slab + PAIRS))

    bottom, twist = ext(PLANES - 2), ext(PLANES - 1)
    own_lanes = lane_ids(ROWS)

    def finish(comp, slab, new):
        for half in range(2):
            level = slab + half * PAIRS
            value = block_ref[comp, level]
            value = jnp.where(own_lanes < 8, turned(-8 - 64 * half)(new), value)
            out_ref[comp, level] = jnp.where(own_lanes >= 120, turned(120 - 32 - 64 * half)(new), value)

    evolve(
        scratch, PAIRS, True, plain_of, strip(COMPS * PAIRS, bottom, bottom), strip(COMPS * PAIRS + 1, twist, twist), finish
    )


def call(kernel, out_shape, scratch, flops, moved, *operands, whole=False):
    far = pltpu.HBM if whole else pltpu.VMEM
    places = [pltpu.SMEM if operand.shape == (1,) else far for operand in operands]
    return pl.pallas_call(
        kernel,
        out_shape=out_shape,
        in_specs=[pl.BlockSpec(memory_space=place) for place in places],
        out_specs=jax.tree.map(lambda _: pl.BlockSpec(memory_space=pltpu.VMEM), out_shape),
        scratch_shapes=scratch,
        compiler_params=pltpu.CompilerParams(vmem_limit_bytes=(LIMIT if whole else 24) << 20),
        cost_estimate=pl.CostEstimate(flops=flops, bytes_accessed=moved, transcendentals=0),
    )(*operands)


def scratch_for(slabs):
    rows = lambda planes: pltpu.VMEM((planes * PITCH, LANES), jnp.float32)
    return (rows(COMPS * slabs),) * 5 + (rows(slabs),) * 2 + (rows(2),) * 2 + (pltpu.VMEM((2 * LANES, 2 * LANES), jnp.bfloat16),)


def local(fields, sea_mask, bottom_level, coriolis):
    del sea_mask
    lat_count, lon_count = lax.axis_size("lat"), lax.axis_size("lon")
    lat = lax.axis_index("lat").astype(jnp.int32).reshape(1)
    lon = lax.axis_index("lon").astype(jnp.int32).reshape(1)
    axes = ("lon", "lat")
    index_of = lambda lon, row: (lon % lon_count) * lat_count + row
    f32 = lambda *shape: jax.ShapeDtypeStruct(shape, jnp.float32)

    def other_side(i):
        return ((i + 1) ^ 1) - 1

    everywhere = [(i, j) for i in range(lon_count) for j in range(lat_count)]
    lat_first = [(index_of(i, j), index_of(i, j ^ 1)) for i, j in everywhere]
    lat_second = []
    for i, j in everywhere:
        if j == lat_count - 1:
            lat_second.append((index_of(i, j), index_of(lon_count - 1 - i, j)))
        elif j > 0:
            lat_second.append((index_of(i, j), index_of(i, other_side(j))))
    lon_first = [(index_of(i, j), index_of(i ^ 1, j)) for i, j in everywhere]
    lon_second = [(index_of(i, j), index_of(other_side(i), j)) for i, j in everywhere]

    flat = jnp.stack([bottom_level.astype(jnp.float32), coriolis])
    rows_message, side_message = f32(PLANES, HALO, LANES), f32(GROUPS, EXT, LANES)
    held = (
        pltpu.VMEM((COMPS, LEVELS, HALO, LANES), jnp.float32), pltpu.VMEM((HALO, LANES), jnp.int32),
        pltpu.VMEM((HALO, LANES), jnp.float32), pltpu.SemaphoreType.DMA((3,)),
    )
    to_second = call(
        functools.partial(pack_second_kernel, lat_count=lat_count), f32(PLANES + 1, HALO, LANES), held, 10**5, 10**6,
        lat, fields, bottom_level, coriolis, whole=True,
    )
    second = lax.ppermute(to_second, axes, lat_second)
    to_first = call(pack_first_kernel, rows_message, (), 10**5, 10**6, lat, fields, flat)
    first = lax.ppermute(to_first, axes, lat_first)
    to_second_side, to_first_side = call(
        pack_sides_kernel, (side_message,) * 2, (), 10**5, 10**6, lat, lon, fields, flat, second, first
    )
    second_side = lax.ppermute(to_second_side, axes, lon_second)
    first_side = lax.ppermute(to_first_side, axes, lon_first)
    result = f32(COMPS, LEVELS, ROWS, LANES)
    block = call(block_kernel, result, scratch_for(LEVELS), 10**9, 10**6, lat, fields, flat, second, first)
    return call(
        strips_kernel, result, scratch_for(PAIRS), 10**8, 10**6,
        lat, lon, fields, flat, second, first, second_side, first_side, block,
    )


def solution(mesh):
    in_specs = (P(None, None, "lat", "lon"), P(None, "lat", "lon"), P("lat", "lon"), P("lat", "lon"))
    out_specs = P(None, None, "lat", "lon")
    return jax.shard_map(local, mesh=mesh, in_specs=in_specs, out_specs=out_specs, check_vma=False)
```

```python
import functools

import jax
import jax.numpy as jnp
from jax import lax
from jax.experimental import pallas as pl
from jax.experimental.pallas import tpu as pltpu
from jax.sharding import PartitionSpec as P

STEPS = 4
STEP_DT = 0.1
KAPPA = 0.2
DRAG_RATE = 0.5
GRAVITY = 0.1
ALPHA_T = 0.2
BETA_S = 0.15

COMPS = 4
LEVELS = 10
PAIRS = LEVELS // 2
PLANES = COMPS * LEVELS + 2
ROWS = 16
HALO = 8
EXT = ROWS + 2 * HALO
EARLY = ROWS + HALO
SPARE = 48
PITCH = EXT + 16
LANES = 128
BATCH = 5
LAG = 1
LIMIT = 56
GROUPS = 3


def lane_ids(rows):
    return lax.broadcasted_iota(jnp.int32, (rows, LANES), 1)


def turned(by):
    if by % LANES == 0:
        return lambda value: value
    return lambda value: pltpu.roll(value, by % LANES, 1)


def beside(value):
    return turned(-1)(value) + turned(1)(value)


def sloped(value):
    return turned(-2)(value) - turned(2)(value)


def in_two(value):
    high = value.astype(jnp.bfloat16)
    low = (value - high.astype(jnp.float32)).astype(jnp.bfloat16)
    return jnp.concatenate([high, low], axis=1)


def neighbours():
    source = lax.broadcasted_iota(jnp.int32, (2 * LANES, 2 * LANES), 0) % LANES
    target = lax.broadcasted_iota(jnp.int32, (2 * LANES, 2 * LANES), 1)
    east = (source - target) % LANES
    sums = jnp.where((east == 1) | (east == LANES - 1), 1.0, 0.0)
    slopes = jnp.where(east == 2, 1.0, jnp.where(east == LANES - 2, -1.0, 0.0))
    return jnp.where(target < LANES, sums, slopes).astype(jnp.bfloat16)


def pairs_of(plane_of):
    for index in range(COMPS * PAIRS + 2):
        comp, level = divmod(index, PAIRS)
        if comp < COMPS:
            low = plane_of(comp * LEVELS + level)
            yield index, low, plane_of(comp * LEVELS + level + PAIRS)
        else:
            value = plane_of(COMPS * LEVELS + index - COMPS * PAIRS)
            yield index, value, value


def plane_reader(fields_ref, flat_ref):
    def read(plane, start, rows):
        if plane >= COMPS * LEVELS:
            return flat_ref[plane - COMPS * LEVELS, pl.ds(start, rows), :]
        return fields_ref[plane // LEVELS, plane % LEVELS, pl.ds(start, rows), :]

    return read


def folded(value, lanes):
    rows = HALO - 1 - lax.broadcasted_iota(jnp.int32, (HALO, LANES), 0)
    return jnp.take_along_axis(jnp.take_along_axis(value, lanes, axis=1), rows, axis=0)


def pack_second_kernel(
    lat_ref, fields_any, bottom_any, coriolis_any, second_ref, rows_ref, bottom_ref, coriolis_ref, semaphores, *, lat_count
):
    lat = lat_ref[0]
    row = pl.multiple_of(jnp.where(lat % 2 == 0, 0, HALO), HALO)
    here = pl.ds(row, HALO)
    copies = [
        pltpu.make_async_copy(source, target, semaphores.at[index])
        for index, (source, target) in enumerate((
            (fields_any.at[:, :, here, :], rows_ref),
            (bottom_any.at[here, :], bottom_ref),
            (coriolis_any.at[here, :], coriolis_ref),
        ))
    ]
    for copy in copies:
        copy.start()
    for copy in copies:
        copy.wait()

    def read(plane):
        if plane < COMPS * LEVELS:
            return rows_ref[plane // LEVELS, plane % LEVELS]
        return bottom_ref[...].astype(jnp.float32) if plane == PLANES - 2 else coriolis_ref[...]

    second_ref[PLANES] = jnp.zeros((HALO, LANES), jnp.float32)

    @pl.when(lat < lat_count - 1)
    def _():
        for plane in range(PLANES):
            second_ref[plane] = read(plane)

    @pl.when(lat == lat_count - 1)
    def _():
        back = LANES - 1 - lane_ids(HALO)
        for plane in range(PLANES):
            value = folded(read(plane), back)
            second_ref[plane] = -value if 2 * LEVELS <= plane < 4 * LEVELS else value


def pack_first_kernel(lat_ref, fields_ref, flat_ref, first_ref):
    read = plane_reader(fields_ref, flat_ref)
    row = pl.multiple_of(jnp.where(lat_ref[0] % 2 == 0, HALO, 0), HALO)
    for plane in range(PLANES):
        first_ref[plane] = read(plane, row, HALO)


def side_tiles(rows, plane_of, shift):
    lanes = lane_ids(rows)
    tiles = [jnp.zeros((rows, LANES), jnp.float32) for _ in range(GROUPS)]
    for index, low, high in pairs_of(plane_of):
        group, slot = divmod(index, 8)
        for at, value in ((8 * slot, low), (8 * slot + 64, high)):
            here = (lanes >= at) & (lanes < at + 8)
            tiles[group] = jnp.where(here, pltpu.roll(value, at + shift, 1), tiles[group])
    return tiles


def pack_early_kernel(lat_ref, lon_ref, fields_ref, flat_ref, first_ref, second_side_ref, first_side_ref):
    read = plane_reader(fields_ref, flat_ref)
    lat_even, lon_even = lat_ref[0] % 2 == 0, lon_ref[0] % 2 == 0

    def early(plane):
        own, halo = read(plane, 0, ROWS), first_ref[plane]
        top = jnp.where(lat_even, own[:HALO], halo)
        middle = jnp.where(lat_even, own[HALO:], own[:HALO])
        return jnp.concatenate([top, middle, jnp.where(lat_even, halo, own[HALO:])], axis=0)

    for ref, shift in (
        (second_side_ref, jnp.where(lon_even, 0, HALO)), (first_side_ref, jnp.where(lon_even, HALO, 0))
    ):
        for group, tile in enumerate(side_tiles(EARLY, early, shift)):
            ref[group, pl.ds(0, EARLY), :] = tile
    for group in range(GROUPS):
        for row in range(EARLY, SPARE, 8):
            second_side_ref[group, pl.ds(row, 8), :] = jnp.zeros((8, LANES), jnp.float32)


def pack_late_kernel(lon_ref, second_ref, second_early_ref, first_early_ref, second_side_ref, first_side_ref):
    lon_even = lon_ref[0] % 2 == 0
    for out_ref, early_ref, shift in (
        (second_side_ref, second_early_ref, jnp.where(lon_even, 0, HALO)),
        (first_side_ref, first_early_ref, jnp.where(lon_even, HALO, 0)),
    ):
        for group, tile in enumerate(side_tiles(HALO, lambda plane: second_ref[plane], shift)):
            out_ref[group, pl.ds(0, EARLY), :] = early_ref[group, pl.ds(0, EARLY), :]
            out_ref[group, pl.ds(EARLY, HALO), :] = tile


def joiner(lat_ref):
    even = lat_ref[0] % 2 == 0

    def joined(one, own, two):
        return jnp.concatenate([jnp.where(even, two, one), own, jnp.where(even, one, two)], axis=0)

    return joined


def evolve(scratch, slabs, strips, plain_of, bottom, twist, finish):
    raw, state, lap, east_diff, north_diff, wet, count, flat, press, matrix = scratch

    def at(slab, comp=0):
        return (comp * slabs + slab) * PITCH + 8

    def get(ref, start, rows):
        return ref[pl.ds(start, rows), :]

    def put(ref, start, value):
        ref[pl.ds(start, value.shape[0]), :] = value

    matrix[...] = neighbours()
    if strips:
        bottom = bottom - jnp.where(lane_ids(EXT) >= 64, float(PAIRS), 0.0)
    put(flat, 8, bottom)
    put(flat, PITCH + 8, STEP_DT * twist)
    for slab in range(slabs):
        value = jnp.where(bottom > float(slab), 1.0, 0.0)
        put(wet, at(slab), value)
        around = (get(wet, at(slab) - 1, EXT) + get(wet, at(slab) + 1, EXT)) + beside(value)
        put(count, at(slab), around)
        for comp in range(COMPS):
            plain = plain_of(comp, slab)
            put(raw, at(slab, comp), plain)
            put(state, at(slab, comp), plain * value)

    a_windows = ((0, EXT), (0, EXT), (4, EXT - 8), (0, EXT))
    b_windows = ((0, EXT), (0, EXT), (4, EXT - 8), (HALO, ROWS))

    def before(step, batch):
        a_row, a_rows = a_windows[step]
        b_row, b_rows = b_windows[step]
        slope_of = raw if step == 0 else state
        fields = [(slab, comp) for slab in batch for comp in range(COMPS)]

        def lateral(ref):
            values = [in_two(get(ref, at(*field) + a_row, a_rows)) for field in fields]
            return jnp.dot(jnp.concatenate(values, axis=0), matrix[...], preferred_element_type=jnp.float32)

        both = lateral(state)
        slopes = lateral(raw) if step == 0 else both
        for index, (slab, comp) in enumerate(fields):
            w = get(wet, at(slab) + a_row, a_rows)
            n = get(count, at(slab) + a_row, a_rows)
            start = at(slab, comp)
            value = get(state, start + a_row, a_rows)
            along = get(state, start + a_row + 1, a_rows) + get(state, start + a_row - 1, a_rows)
            sums = both[index * a_rows : (index + 1) * a_rows, :LANES]
            put(lap, start + a_row, w * (along + sums - n * value))
            first = index * a_rows + b_row - a_row
            put(east_diff, start + b_row, slopes[first : first + b_rows, LANES:])
            put(north_diff, start + b_row, get(slope_of, start + b_row + 2, b_rows) - get(slope_of, start + b_row - 2, b_rows))

    scale = 0.5 * STEP_DT * GRAVITY

    def heavier(ref, slab, row, rows):
        return (scale * BETA_S) * get(ref, at(slab, 1) + row, rows) - (scale * ALPHA_T) * get(ref, at(slab, 0) + row, rows)

    def base(step):
        row, rows = b_windows[step]
        for slot, ref in enumerate((east_diff, north_diff)):
            total = None
            for slab in range(slabs):
                term = heavier(ref, slab, row, rows)
                total = term if total is None else total + term
            put(press, slot * PITCH + 8 + row, jnp.where(lane_ids(rows) >= 64, turned(64)(total), 0.0))

    def after(step, slab):
        row, rows = b_windows[step]
        w = get(wet, at(slab) + row, rows)
        n = get(count, at(slab) + row, rows)
        slopes = []
        for slot, ref in enumerate((east_diff, north_diff)):
            slope = heavier(ref, slab, row, rows)
            press_at = slot * PITCH + 8 + row
            if slab > 0 or strips:
                slope = slope + get(press, press_at, rows)
            put(press, press_at, slope)
            slopes.append(slope)
        twist_b = get(flat, PITCH + 8 + row, rows)
        bottom_b = get(flat, 8 + row, rows)
        keep = jnp.where(bottom_b == float(slab + 1), 1.0 - STEP_DT * DRAG_RATE, 1.0)
        old_zonal = get(state, at(slab, 2) + row, rows)
        old_merid = get(state, at(slab, 3) + row, rows)
        zonal = (-0.5 * STEP_DT) * old_zonal
        merid = (-0.5 * STEP_DT) * old_merid
        for comp in range(COMPS):
            start = at(slab, comp) + row
            value = get(lap, start, rows)
            along = get(lap, start + 1, rows) + get(lap, start - 1, rows)
            smooth = along + beside(value) - n * value
            new = zonal * get(east_diff, start, rows) + merid * get(north_diff, start, rows) - (STEP_DT * KAPPA) * smooth
            if comp < 2:
                new = new + get(state, start, rows)
            elif comp == 2:
                new = new + (keep * old_zonal + twist_b * old_merid - slopes[0])
            else:
                new = new + (keep * old_merid - twist_b * old_zonal - slopes[1])
            new = w * new
            if step < STEPS - 1:
                put(state, start, new)
            else:
                finish(comp, slab, new)

    batches = [tuple(range(first, min(first + BATCH, slabs))) for first in range(0, slabs, BATCH)]
    for batch in batches:
        before(0, batch)
    for step in range(STEPS):
        if strips:
            base(step)
        waiting = []
        for batch in batches:
            for slab in batch:
                after(step, slab)
            waiting.append(batch)
            if step < STEPS - 1 and len(waiting) > LAG:
                before(step + 1, waiting.pop(0))
        if step < STEPS - 1:
            for batch in waiting:
                before(step + 1, batch)


def block_kernel(lat_ref, fields_ref, flat_ref, second_ref, first_ref, out_ref, *scratch):
    read, joined = plane_reader(fields_ref, flat_ref), joiner(lat_ref)

    def ext(plane):
        return joined(first_ref[plane], read(plane, 0, ROWS), second_ref[plane])

    def finish(comp, slab, new):
        out_ref[comp, slab] = new

    evolve(
        scratch, LEVELS, False, lambda comp, slab: ext(comp * LEVELS + slab), ext(PLANES - 2), ext(PLANES - 1), finish
    )


def strips_kernel(
    lat_ref, lon_ref, fields_ref, flat_ref, second_ref, first_ref, sent_ref, early_ref, second_side_ref, first_side_ref, block_ref,
    out_ref, *scratch, lat_count, lon_count,
):
    read, joined = plane_reader(fields_ref, flat_ref), joiner(lat_ref)
    lanes = lane_ids(EXT)
    upper = lanes >= 64
    place = lanes % 64
    lat, lon = lat_ref[0], lon_ref[0]
    lat_even, lon_even = lat % 2 == 0, lon % 2 == 0

    def ext(plane):
        return joined(first_ref[plane], read(plane, 0, ROWS), second_ref[plane])

    other = (jnp.where(lon_even, lon - 1, lon + 1) + lon_count) % lon_count
    seam = (lat == lat_count - 1) & (other == lon_count - 1 - lon)
    back = lane_ids(HALO) + 7 - 2 * (lane_ids(HALO) % 8)

    def in_order(value):
        early, late = value[:EARLY], value[EARLY:]
        return jnp.where(lat_even, jnp.concatenate([late, early], axis=0), jnp.concatenate([early, late], axis=0))

    from_west, from_east = [], []
    for group in range(GROUPS):
        index = 8 * group + lane_ids(HALO) % 64 // 8
        sign = jnp.where((index >= 2 * PAIRS) & (index < 4 * PAIRS), -1.0, 1.0)
        own = sign * folded(sent_ref[group, pl.ds(2 * HALO, HALO), :], back)
        at_seam = jnp.concatenate([early_ref[group, pl.ds(0, EARLY), :], own], axis=0)
        second = in_order(jnp.where(seam, at_seam, second_side_ref[group]))
        first = in_order(first_side_ref[group])
        from_west.append(jnp.where(lon_even, second, first))
        from_east.append(jnp.where(lon_even, first, second))

    def strip(index, low, high):
        group, slot = divmod(index, 8)
        value = jnp.where(upper, turned(64 + 8)(high), turned(8)(low))
        value = jnp.where((place >= 24) & (place < 40), jnp.where(upper, turned(64 + 40)(high), turned(40)(low)), value)
        value = jnp.where(place < 8, turned(-8 * slot)(from_west[group]), value)
        value = jnp.where((place >= 40) & (place < 48), turned(40 - 8 * slot)(from_east[group]), value)
        return value

    def plain_of(comp, slab):
        return strip(comp * PAIRS + slab, ext(comp * LEVELS + slab), ext(comp * LEVELS + slab + PAIRS))

    bottom, twist = ext(PLANES - 2), ext(PLANES - 1)
    own_lanes = lane_ids(ROWS)

    def finish(comp, slab, new):
        for half in range(2):
            level = slab + half * PAIRS
            value = block_ref[comp, level]
            value = jnp.where(own_lanes < 8, turned(-8 - 64 * half)(new), value)
            out_ref[comp, level] = jnp.where(own_lanes >= 120, turned(120 - 32 - 64 * half)(new), value)

    evolve(
        scratch, PAIRS, True, plain_of, strip(COMPS * PAIRS, bottom, bottom), strip(COMPS * PAIRS + 1, twist, twist), finish
    )


def call(kernel, out_shape, scratch, flops, moved, *operands, whole=False):
    far = pltpu.HBM if whole else pltpu.VMEM
    places = [pltpu.SMEM if operand.shape == (1,) else far for operand in operands]
    return pl.pallas_call(
        kernel,
        out_shape=out_shape,
        in_specs=[pl.BlockSpec(memory_space=place) for place in places],
        out_specs=jax.tree.map(lambda _: pl.BlockSpec(memory_space=pltpu.VMEM), out_shape),
        scratch_shapes=scratch,
        compiler_params=pltpu.CompilerParams(vmem_limit_bytes=(LIMIT if whole else 24) << 20),
        cost_estimate=pl.CostEstimate(flops=flops, bytes_accessed=moved, transcendentals=0),
    )(*operands)


def scratch_for(slabs):
    rows = lambda planes: pltpu.VMEM((planes * PITCH, LANES), jnp.float32)
    return (rows(COMPS * slabs),) * 5 + (rows(slabs),) * 2 + (rows(2),) * 2 + (pltpu.VMEM((2 * LANES, 2 * LANES), jnp.bfloat16),)


def local(fields, sea_mask, bottom_level, coriolis):
    del sea_mask
    lat_count, lon_count = lax.axis_size("lat"), lax.axis_size("lon")
    lat = lax.axis_index("lat").astype(jnp.int32).reshape(1)
    lon = lax.axis_index("lon").astype(jnp.int32).reshape(1)
    axes = ("lon", "lat")
    index_of = lambda lon, row: (lon % lon_count) * lat_count + row
    f32 = lambda *shape: jax.ShapeDtypeStruct(shape, jnp.float32)

    def other_side(i):
        return ((i + 1) ^ 1) - 1

    everywhere = [(i, j) for i in range(lon_count) for j in range(lat_count)]
    lat_first = [(index_of(i, j), index_of(i, j ^ 1)) for i, j in everywhere]
    lat_second = []
    for i, j in everywhere:
        if j == lat_count - 1:
            lat_second.append((index_of(i, j), index_of(lon_count - 1 - i, j)))
        elif j > 0:
            lat_second.append((index_of(i, j), index_of(i, other_side(j))))
    lon_first = [(index_of(i, j), index_of(i ^ 1, j)) for i, j in everywhere]
    lon_second = [(index_of(i, j), index_of(other_side(i), j)) for i, j in everywhere]
    at_seam = [j == lat_count - 1 and other_side(i) % lon_count == lon_count - 1 - i for i, j in everywhere]
    lon_early = [pair for pair, seam in zip(lon_second, at_seam, strict=True) if seam]
    lon_late = [pair for pair, seam in zip(lon_second, at_seam, strict=True) if not seam]

    flat = jnp.stack([bottom_level.astype(jnp.float32), coriolis])
    rows_message = f32(PLANES, HALO, LANES)
    held = (
        pltpu.VMEM((COMPS, LEVELS, HALO, LANES), jnp.float32), pltpu.VMEM((HALO, LANES), jnp.int32),
        pltpu.VMEM((HALO, LANES), jnp.float32), pltpu.SemaphoreType.DMA((3,)),
    )
    to_second = call(
        functools.partial(pack_second_kernel, lat_count=lat_count), f32(PLANES + 1, HALO, LANES), held, 10**5, 10**6,
        lat, fields, bottom_level, coriolis, whole=True,
    )
    second = lax.ppermute(to_second, axes, lat_second)
    to_first = call(pack_first_kernel, rows_message, (), 10**5, 10**6, lat, fields, flat)
    first = lax.ppermute(to_first, axes, lat_first)
    to_second_early, to_first_early = call(
        pack_early_kernel, (f32(GROUPS, SPARE, LANES), f32(GROUPS, EARLY, LANES)), (), 10**5, 10**6,
        lat, lon, fields, flat, first,
    )
    early = lax.ppermute(to_second_early, axes, lon_early)
    to_second_side, to_first_side = call(
        pack_late_kernel, (f32(GROUPS, EXT, LANES),) * 2, (), 10**5, 10**6, lon, second, to_second_early, to_first_early
    )
    second_side = lax.ppermute(to_second_side, axes, lon_late)
    first_side = lax.ppermute(to_first_side, axes, lon_first)
    result = f32(COMPS, LEVELS, ROWS, LANES)
    block = call(block_kernel, result, scratch_for(LEVELS), 10**9, 10**6, lat, fields, flat, second, first)
    return call(
        functools.partial(strips_kernel, lat_count=lat_count, lon_count=lon_count), result, scratch_for(PAIRS), 10**8, 10**6,
        lat, lon, fields, flat, second, first, to_second_early, early, second_side, first_side, block,
    )


def solution(mesh):
    in_specs = (P(None, None, "lat", "lon"), P(None, "lat", "lon"), P("lat", "lon"), P("lat", "lon"))
    out_specs = P(None, None, "lat", "lon")
    return jax.shard_map(local, mesh=mesh, in_specs=in_specs, out_specs=out_specs, check_vma=False)
```

```python
import functools

import jax
import jax.numpy as jnp
from jax import lax
from jax.experimental import pallas as pl
from jax.experimental.pallas import tpu as pltpu
from jax.sharding import PartitionSpec as P

STEPS = 4
STEP_DT = 0.1
KAPPA = 0.2
DRAG_RATE = 0.5
GRAVITY = 0.1
ALPHA_T = 0.2
BETA_S = 0.15

COMPS = 4
LEVELS = 10
PAIRS = LEVELS // 2
PLANES = COMPS * LEVELS + 2
ROWS = 16
HALO = 8
EXT = ROWS + 2 * HALO
EARLY = ROWS + HALO
SPARE = 48
PITCH = EXT + 16
LANES = 128
BATCH = 5
LAG = 1
GROUPS = 3


def lane_ids(rows):
    return lax.broadcasted_iota(jnp.int32, (rows, LANES), 1)


def turned(by):
    if by % LANES == 0:
        return lambda value: value
    return lambda value: pltpu.roll(value, by % LANES, 1)


def beside(value):
    return turned(-1)(value) + turned(1)(value)


def sloped(value):
    return turned(-2)(value) - turned(2)(value)


def in_two(value):
    high = value.astype(jnp.bfloat16)
    low = (value - high.astype(jnp.float32)).astype(jnp.bfloat16)
    return jnp.concatenate([high, low], axis=1)


def neighbours():
    source = lax.broadcasted_iota(jnp.int32, (2 * LANES, 2 * LANES), 0) % LANES
    target = lax.broadcasted_iota(jnp.int32, (2 * LANES, 2 * LANES), 1)
    east = (source - target) % LANES
    sums = jnp.where((east == 1) | (east == LANES - 1), 1.0, 0.0)
    slopes = jnp.where(east == 2, 1.0, jnp.where(east == LANES - 2, -1.0, 0.0))
    return jnp.where(target < LANES, sums, slopes).astype(jnp.bfloat16)


def pairs_of(plane_of):
    for index in range(COMPS * PAIRS + 2):
        comp, level = divmod(index, PAIRS)
        if comp < COMPS:
            low = plane_of(comp * LEVELS + level)
            yield index, low, plane_of(comp * LEVELS + level + PAIRS)
        else:
            value = plane_of(COMPS * LEVELS + index - COMPS * PAIRS)
            yield index, value, value


def plane_reader(fields_ref, flat_ref):
    def read(plane, start, rows):
        if plane >= COMPS * LEVELS:
            return flat_ref[plane - COMPS * LEVELS, pl.ds(start, rows), :]
        return fields_ref[plane // LEVELS, plane % LEVELS, pl.ds(start, rows), :]

    return read


def folded(value, lanes):
    rows = HALO - 1 - lax.broadcasted_iota(jnp.int32, (HALO, LANES), 0)
    return jnp.take_along_axis(jnp.take_along_axis(value, lanes, axis=1), rows, axis=0)


def pack_first_kernel(lat_ref, fields_ref, flat_ref, first_ref):
    read = plane_reader(fields_ref, flat_ref)
    row = pl.multiple_of(jnp.where(lat_ref[0] % 2 == 0, HALO, 0), HALO)
    for plane in range(PLANES):
        first_ref[plane] = read(plane, row, HALO)


def side_tiles(rows, plane_of, shift):
    lanes = lane_ids(rows)
    tiles = [jnp.zeros((rows, LANES), jnp.float32) for _ in range(GROUPS)]
    for index, low, high in pairs_of(plane_of):
        group, slot = divmod(index, 8)
        for at, value in ((8 * slot, low), (8 * slot + 64, high)):
            here = (lanes >= at) & (lanes < at + 8)
            tiles[group] = jnp.where(here, pltpu.roll(value, at + shift, 1), tiles[group])
    return tiles


def pack_early_kernel(lat_ref, lon_ref, fields_ref, flat_ref, first_ref, second_side_ref, first_side_ref):
    read = plane_reader(fields_ref, flat_ref)
    lat_even, lon_even = lat_ref[0] % 2 == 0, lon_ref[0] % 2 == 0

    def early(plane):
        own, halo = read(plane, 0, ROWS), first_ref[plane]
        top = jnp.where(lat_even, own[:HALO], halo)
        middle = jnp.where(lat_even, own[HALO:], own[:HALO])
        return jnp.concatenate([top, middle, jnp.where(lat_even, halo, own[HALO:])], axis=0)

    for ref, shift in (
        (second_side_ref, jnp.where(lon_even, 0, HALO)), (first_side_ref, jnp.where(lon_even, HALO, 0))
    ):
        for group, tile in enumerate(side_tiles(EARLY, early, shift)):
            ref[group, pl.ds(0, EARLY), :] = tile
    for group in range(GROUPS):
        for row in range(EARLY, SPARE, 8):
            second_side_ref[group, pl.ds(row, 8), :] = jnp.zeros((8, LANES), jnp.float32)


def pack_late_kernel(
    lat_ref, lon_ref, received_ref, second_early_ref, first_early_ref, second_ref, second_side_ref, first_side_ref, *, lat_count
):
    lat, lon_even = lat_ref[0], lon_ref[0] % 2 == 0

    @pl.when(lat < lat_count - 1)
    def _():
        for plane in range(PLANES):
            second_ref[plane] = received_ref[plane]

    @pl.when(lat == lat_count - 1)
    def _():
        back = LANES - 1 - lane_ids(HALO)
        for plane in range(PLANES):
            value = folded(received_ref[plane], back)
            second_ref[plane] = -value if 2 * LEVELS <= plane < 4 * LEVELS else value

    for out_ref, early_ref, shift in (
        (second_side_ref, second_early_ref, jnp.where(lon_even, 0, HALO)),
        (first_side_ref, first_early_ref, jnp.where(lon_even, HALO, 0)),
    ):
        for group, tile in enumerate(side_tiles(HALO, lambda plane: second_ref[plane], shift)):
            out_ref[group, pl.ds(0, EARLY), :] = early_ref[group, pl.ds(0, EARLY), :]
            out_ref[group, pl.ds(EARLY, HALO), :] = tile


def joiner(lat_ref):
    even = lat_ref[0] % 2 == 0

    def joined(one, own, two):
        return jnp.concatenate([jnp.where(even, two, one), own, jnp.where(even, one, two)], axis=0)

    return joined


def evolve(scratch, slabs, strips, plain_of, bottom, twist, finish):
    raw, state, lap, east_diff, north_diff, wet, count, flat, press, matrix = scratch

    def at(slab, comp=0):
        return (comp * slabs + slab) * PITCH + 8

    def get(ref, start, rows):
        return ref[pl.ds(start, rows), :]

    def put(ref, start, value):
        ref[pl.ds(start, value.shape[0]), :] = value

    matrix[...] = neighbours()
    if strips:
        bottom = bottom - jnp.where(lane_ids(EXT) >= 64, float(PAIRS), 0.0)
    put(flat, 8, bottom)
    put(flat, PITCH + 8, STEP_DT * twist)
    for slab in range(slabs):
        value = jnp.where(bottom > float(slab), 1.0, 0.0)
        put(wet, at(slab), value)
        around = (get(wet, at(slab) - 1, EXT) + get(wet, at(slab) + 1, EXT)) + beside(value)
        put(count, at(slab), around)
        for comp in range(COMPS):
            plain = plain_of(comp, slab)
            put(raw, at(slab, comp), plain)
            put(state, at(slab, comp), plain * value)

    a_windows = ((0, EXT), (0, EXT), (4, EXT - 8), (0, EXT))
    b_windows = ((0, EXT), (0, EXT), (4, EXT - 8), (HALO, ROWS))

    def before(step, batch):
        a_row, a_rows = a_windows[step]
        b_row, b_rows = b_windows[step]
        slope_of = raw if step == 0 else state
        fields = [(slab, comp) for slab in batch for comp in range(COMPS)]

        def lateral(ref):
            values = [in_two(get(ref, at(*field) + a_row, a_rows)) for field in fields]
            return jnp.dot(jnp.concatenate(values, axis=0), matrix[...], preferred_element_type=jnp.float32)

        both = lateral(state)
        slopes = lateral(raw) if step == 0 else both
        for index, (slab, comp) in enumerate(fields):
            w = get(wet, at(slab) + a_row, a_rows)
            n = get(count, at(slab) + a_row, a_rows)
            start = at(slab, comp)
            value = get(state, start + a_row, a_rows)
            along = get(state, start + a_row + 1, a_rows) + get(state, start + a_row - 1, a_rows)
            sums = both[index * a_rows : (index + 1) * a_rows, :LANES]
            put(lap, start + a_row, w * (along + sums - n * value))
            first = index * a_rows + b_row - a_row
            put(east_diff, start + b_row, slopes[first : first + b_rows, LANES:])
            put(north_diff, start + b_row, get(slope_of, start + b_row + 2, b_rows) - get(slope_of, start + b_row - 2, b_rows))

    scale = 0.5 * STEP_DT * GRAVITY

    def heavier(ref, slab, row, rows):
        return (scale * BETA_S) * get(ref, at(slab, 1) + row, rows) - (scale * ALPHA_T) * get(ref, at(slab, 0) + row, rows)

    def base(step):
        row, rows = b_windows[step]
        for slot, ref in enumerate((east_diff, north_diff)):
            total = None
            for slab in range(slabs):
                term = heavier(ref, slab, row, rows)
                total = term if total is None else total + term
            put(press, slot * PITCH + 8 + row, jnp.where(lane_ids(rows) >= 64, turned(64)(total), 0.0))

    def after(step, slab):
        row, rows = b_windows[step]
        w = get(wet, at(slab) + row, rows)
        n = get(count, at(slab) + row, rows)
        slopes = []
        for slot, ref in enumerate((east_diff, north_diff)):
            slope = heavier(ref, slab, row, rows)
            press_at = slot * PITCH + 8 + row
            if slab > 0 or strips:
                slope = slope + get(press, press_at, rows)
            put(press, press_at, slope)
            slopes.append(slope)
        twist_b = get(flat, PITCH + 8 + row, rows)
        bottom_b = get(flat, 8 + row, rows)
        keep = jnp.where(bottom_b == float(slab + 1), 1.0 - STEP_DT * DRAG_RATE, 1.0)
        old_zonal = get(state, at(slab, 2) + row, rows)
        old_merid = get(state, at(slab, 3) + row, rows)
        zonal = (-0.5 * STEP_DT) * old_zonal
        merid = (-0.5 * STEP_DT) * old_merid
        for comp in range(COMPS):
            start = at(slab, comp) + row
            value = get(lap, start, rows)
            along = get(lap, start + 1, rows) + get(lap, start - 1, rows)
            smooth = along + beside(value) - n * value
            new = zonal * get(east_diff, start, rows) + merid * get(north_diff, start, rows) - (STEP_DT * KAPPA) * smooth
            if comp < 2:
                new = new + get(state, start, rows)
            elif comp == 2:
                new = new + (keep * old_zonal + twist_b * old_merid - slopes[0])
            else:
                new = new + (keep * old_merid - twist_b * old_zonal - slopes[1])
            new = w * new
            if step < STEPS - 1:
                put(state, start, new)
            else:
                finish(comp, slab, new)

    batches = [tuple(range(first, min(first + BATCH, slabs))) for first in range(0, slabs, BATCH)]
    for batch in batches:
        before(0, batch)
    for step in range(STEPS):
        if strips:
            base(step)
        waiting = []
        for batch in batches:
            for slab in batch:
                after(step, slab)
            waiting.append(batch)
            if step < STEPS - 1 and len(waiting) > LAG:
                before(step + 1, waiting.pop(0))
        if step < STEPS - 1:
            for batch in waiting:
                before(step + 1, batch)


def block_kernel(lat_ref, fields_ref, flat_ref, second_ref, first_ref, out_ref, *scratch):
    read, joined = plane_reader(fields_ref, flat_ref), joiner(lat_ref)

    def ext(plane):
        return joined(first_ref[plane], read(plane, 0, ROWS), second_ref[plane])

    def finish(comp, slab, new):
        out_ref[comp, slab] = new

    evolve(
        scratch, LEVELS, False, lambda comp, slab: ext(comp * LEVELS + slab), ext(PLANES - 2), ext(PLANES - 1), finish
    )


def strips_kernel(
    lat_ref, lon_ref, fields_ref, flat_ref, second_ref, first_ref, sent_ref, early_ref, second_side_ref, first_side_ref, block_ref,
    out_ref, *scratch, lat_count, lon_count,
):
    read, joined = plane_reader(fields_ref, flat_ref), joiner(lat_ref)
    lanes = lane_ids(EXT)
    upper = lanes >= 64
    place = lanes % 64
    lat, lon = lat_ref[0], lon_ref[0]
    lat_even, lon_even = lat % 2 == 0, lon % 2 == 0

    def ext(plane):
        return joined(first_ref[plane], read(plane, 0, ROWS), second_ref[plane])

    other = (jnp.where(lon_even, lon - 1, lon + 1) + lon_count) % lon_count
    seam = (lat == lat_count - 1) & (other == lon_count - 1 - lon)
    back = lane_ids(HALO) + 7 - 2 * (lane_ids(HALO) % 8)

    def in_order(value):
        early, late = value[:EARLY], value[EARLY:]
        return jnp.where(lat_even, jnp.concatenate([late, early], axis=0), jnp.concatenate([early, late], axis=0))

    from_west, from_east = [], []
    for group in range(GROUPS):
        index = 8 * group + lane_ids(HALO) % 64 // 8
        sign = jnp.where((index >= 2 * PAIRS) & (index < 4 * PAIRS), -1.0, 1.0)
        own = sign * folded(sent_ref[group, pl.ds(2 * HALO, HALO), :], back)
        at_seam = jnp.concatenate([early_ref[group, pl.ds(0, EARLY), :], own], axis=0)
        second = in_order(jnp.where(seam, at_seam, second_side_ref[group]))
        first = in_order(first_side_ref[group])
        from_west.append(jnp.where(lon_even, second, first))
        from_east.append(jnp.where(lon_even, first, second))

    def strip(index, low, high):
        group, slot = divmod(index, 8)
        value = jnp.where(upper, turned(64 + 8)(high), turned(8)(low))
        value = jnp.where((place >= 24) & (place < 40), jnp.where(upper, turned(64 + 40)(high), turned(40)(low)), value)
        value = jnp.where(place < 8, turned(-8 * slot)(from_west[group]), value)
        value = jnp.where((place >= 40) & (place < 48), turned(40 - 8 * slot)(from_east[group]), value)
        return value

    def plain_of(comp, slab):
        return strip(comp * PAIRS + slab, ext(comp * LEVELS + slab), ext(comp * LEVELS + slab + PAIRS))

    bottom, twist = ext(PLANES - 2), ext(PLANES - 1)
    own_lanes = lane_ids(ROWS)

    def finish(comp, slab, new):
        for half in range(2):
            level = slab + half * PAIRS
            value = block_ref[comp, level]
            value = jnp.where(own_lanes < 8, turned(-8 - 64 * half)(new), value)
            out_ref[comp, level] = jnp.where(own_lanes >= 120, turned(120 - 32 - 64 * half)(new), value)

    evolve(
        scratch, PAIRS, True, plain_of, strip(COMPS * PAIRS, bottom, bottom), strip(COMPS * PAIRS + 1, twist, twist), finish
    )


def call(kernel, out_shape, scratch, flops, moved, *operands):
    places = [pltpu.SMEM if operand.shape == (1,) else pltpu.VMEM for operand in operands]
    return pl.pallas_call(
        kernel,
        out_shape=out_shape,
        in_specs=[pl.BlockSpec(memory_space=place) for place in places],
        out_specs=jax.tree.map(lambda _: pl.BlockSpec(memory_space=pltpu.VMEM), out_shape),
        scratch_shapes=scratch,
        compiler_params=pltpu.CompilerParams(vmem_limit_bytes=24 << 20),
        cost_estimate=pl.CostEstimate(flops=flops, bytes_accessed=moved, transcendentals=0),
    )(*operands)


def scratch_for(slabs):
    rows = lambda planes: pltpu.VMEM((planes * PITCH, LANES), jnp.float32)
    return (rows(COMPS * slabs),) * 5 + (rows(slabs),) * 2 + (rows(2),) * 2 + (pltpu.VMEM((2 * LANES, 2 * LANES), jnp.bfloat16),)


def local(fields, sea_mask, bottom_level, coriolis):
    del sea_mask
    lat_count, lon_count = lax.axis_size("lat"), lax.axis_size("lon")
    lat = lax.axis_index("lat").astype(jnp.int32).reshape(1)
    lon = lax.axis_index("lon").astype(jnp.int32).reshape(1)
    axes = ("lon", "lat")
    index_of = lambda lon, row: (lon % lon_count) * lat_count + row
    f32 = lambda *shape: jax.ShapeDtypeStruct(shape, jnp.float32)

    def other_side(i):
        return ((i + 1) ^ 1) - 1

    everywhere = [(i, j) for i in range(lon_count) for j in range(lat_count)]
    lat_first = [(index_of(i, j), index_of(i, j ^ 1)) for i, j in everywhere]
    lat_second = []
    for i, j in everywhere:
        if j == lat_count - 1:
            lat_second.append((index_of(i, j), index_of(lon_count - 1 - i, j)))
        elif j > 0:
            lat_second.append((index_of(i, j), index_of(i, other_side(j))))
    lon_first = [(index_of(i, j), index_of(i ^ 1, j)) for i, j in everywhere]
    lon_second = [(index_of(i, j), index_of(other_side(i), j)) for i, j in everywhere]
    at_seam = [j == lat_count - 1 and other_side(i) % lon_count == lon_count - 1 - i for i, j in everywhere]
    lon_early = [pair for pair, seam in zip(lon_second, at_seam, strict=True) if seam]
    lon_late = [pair for pair, seam in zip(lon_second, at_seam, strict=True) if not seam]

    flat = jnp.stack([bottom_level.astype(jnp.float32), coriolis])

    def half(value, dim, even):
        return jnp.where(
            even, lax.slice_in_dim(value, 0, HALO, axis=dim), lax.slice_in_dim(value, HALO, ROWS, axis=dim)
        )

    even = lat[0] % 2 == 0
    rows, even = lax.optimization_barrier((half(fields, 2, even), even))
    rows_message = f32(PLANES, HALO, LANES)
    to_second = jnp.concatenate([
        rows.reshape(COMPS * LEVELS, HALO, LANES),
        half(bottom_level, 0, even).astype(jnp.float32)[None],
        half(coriolis, 0, even)[None],
        jnp.zeros((1, HALO, LANES), jnp.float32),
    ])
    received = lax.ppermute(to_second, axes, lat_second)
    to_first = call(pack_first_kernel, rows_message, (), 10**5, 10**6, lat, fields, flat)
    first = lax.ppermute(to_first, axes, lat_first)
    to_second_early, to_first_early = call(
        pack_early_kernel, (f32(GROUPS, SPARE, LANES), f32(GROUPS, EARLY, LANES)), (), 10**5, 10**6,
        lat, lon, fields, flat, first,
    )
    early = lax.ppermute(to_second_early, axes, lon_early)
    second, to_second_side, to_first_side = call(
        functools.partial(pack_late_kernel, lat_count=lat_count), (rows_message,) + (f32(GROUPS, EXT, LANES),) * 2, (),
        10**5, 10**6, lat, lon, received, to_second_early, to_first_early,
    )
    second_side = lax.ppermute(to_second_side, axes, lon_late)
    first_side = lax.ppermute(to_first_side, axes, lon_first)
    result = f32(COMPS, LEVELS, ROWS, LANES)
    block = call(block_kernel, result, scratch_for(LEVELS), 10**9, 10**6, lat, fields, flat, second, first)
    return call(
        functools.partial(strips_kernel, lat_count=lat_count, lon_count=lon_count), result, scratch_for(PAIRS), 10**8, 10**6,
        lat, lon, fields, flat, second, first, to_second_early, early, second_side, first_side, block,
    )


def solution(mesh):
    in_specs = (P(None, None, "lat", "lon"), P(None, "lat", "lon"), P("lat", "lon"), P("lat", "lon"))
    out_specs = P(None, None, "lat", "lon")
    return jax.shard_map(local, mesh=mesh, in_specs=in_specs, out_specs=out_specs, check_vma=False)
```

```python
import functools

import jax
import jax.numpy as jnp
from jax import lax
from jax.experimental import pallas as pl
from jax.experimental.pallas import tpu as pltpu
from jax.sharding import PartitionSpec as P

STEPS = 4
STEP_DT = 0.1
KAPPA = 0.2
DRAG_RATE = 0.5
GRAVITY = 0.1
ALPHA_T = 0.2
BETA_S = 0.15

COMPS = 4
LEVELS = 10
PAIRS = LEVELS // 2
PLANES = COMPS * LEVELS + 2
ROWS = 16
HALO = 8
EXT = ROWS + 2 * HALO
EARLY = ROWS + HALO
SPARE = 48
PITCH = EXT + 16
LANES = 128
BATCH = 5
LAG = 1
GROUPS = 3


def lane_ids(rows):
    return lax.broadcasted_iota(jnp.int32, (rows, LANES), 1)


def turned(by):
    if by % LANES == 0:
        return lambda value: value
    return lambda value: pltpu.roll(value, by % LANES, 1)


def beside(value):
    return turned(-1)(value) + turned(1)(value)


def sloped(value):
    return turned(-2)(value) - turned(2)(value)


def in_two(value):
    high = value.astype(jnp.bfloat16)
    low = (value - high.astype(jnp.float32)).astype(jnp.bfloat16)
    return jnp.concatenate([high, low], axis=1)


def neighbours():
    source = lax.broadcasted_iota(jnp.int32, (2 * LANES, 2 * LANES), 0) % LANES
    target = lax.broadcasted_iota(jnp.int32, (2 * LANES, 2 * LANES), 1)
    east = (source - target) % LANES
    sums = jnp.where((east == 1) | (east == LANES - 1), 1.0, 0.0)
    slopes = jnp.where(east == 2, 1.0, jnp.where(east == LANES - 2, -1.0, 0.0))
    return jnp.where(target < LANES, sums, slopes).astype(jnp.bfloat16)


def pairs_of(plane_of):
    for index in range(COMPS * PAIRS + 2):
        comp, level = divmod(index, PAIRS)
        if comp < COMPS:
            low = plane_of(comp * LEVELS + level)
            yield index, low, plane_of(comp * LEVELS + level + PAIRS)
        else:
            value = plane_of(COMPS * LEVELS + index - COMPS * PAIRS)
            yield index, value, value


def plane_reader(fields_ref, flat_ref):
    def read(plane, start, rows):
        if plane >= COMPS * LEVELS:
            return flat_ref[plane - COMPS * LEVELS, pl.ds(start, rows), :]
        return fields_ref[plane // LEVELS, plane % LEVELS, pl.ds(start, rows), :]

    return read


def folded(value, lanes):
    rows = HALO - 1 - lax.broadcasted_iota(jnp.int32, (HALO, LANES), 0)
    return jnp.take_along_axis(jnp.take_along_axis(value, lanes, axis=1), rows, axis=0)


def pack_first_kernel(lat_ref, fields_ref, flat_ref, first_ref):
    read = plane_reader(fields_ref, flat_ref)
    row = pl.multiple_of(jnp.where(lat_ref[0] % 2 == 0, HALO, 0), HALO)
    for plane in range(PLANES):
        first_ref[plane] = read(plane, row, HALO)


def side_tiles(rows, plane_of, shift):
    lanes = lane_ids(rows)
    tiles = [jnp.zeros((rows, LANES), jnp.float32) for _ in range(GROUPS)]
    for index, low, high in pairs_of(plane_of):
        group, slot = divmod(index, 8)
        for at, value in ((8 * slot, low), (8 * slot + 64, high)):
            here = (lanes >= at) & (lanes < at + 8)
            tiles[group] = jnp.where(here, pltpu.roll(value, at + shift, 1), tiles[group])
    return tiles


def pack_early_kernel(lat_ref, lon_ref, fields_ref, flat_ref, first_ref, second_side_ref, first_side_ref):
    read = plane_reader(fields_ref, flat_ref)
    lat_even, lon_even = lat_ref[0] % 2 == 0, lon_ref[0] % 2 == 0

    def early(plane):
        own, halo = read(plane, 0, ROWS), first_ref[plane]
        top = jnp.where(lat_even, own[:HALO], halo)
        middle = jnp.where(lat_even, own[HALO:], own[:HALO])
        return jnp.concatenate([top, middle, jnp.where(lat_even, halo, own[HALO:])], axis=0)

    for ref, shift in (
        (second_side_ref, jnp.where(lon_even, 0, HALO)), (first_side_ref, jnp.where(lon_even, HALO, 0))
    ):
        for group, tile in enumerate(side_tiles(EARLY, early, shift)):
            ref[group, pl.ds(0, EARLY), :] = tile
    for group in range(GROUPS):
        for row in range(EARLY, SPARE, 8):
            second_side_ref[group, pl.ds(row, 8), :] = jnp.zeros((8, LANES), jnp.float32)


def pack_late_kernel(
    lat_ref, lon_ref, received_ref, second_early_ref, first_early_ref, second_ref, second_side_ref, first_side_ref, *, lat_count
):
    lat, lon_even = lat_ref[0], lon_ref[0] % 2 == 0

    @pl.when(lat < lat_count - 1)
    def _():
        for plane in range(PLANES):
            second_ref[plane] = received_ref[plane]

    @pl.when(lat == lat_count - 1)
    def _():
        back = LANES - 1 - lane_ids(HALO)
        for plane in range(PLANES):
            value = folded(received_ref[plane], back)
            second_ref[plane] = -value if 2 * LEVELS <= plane < 4 * LEVELS else value

    for out_ref, early_ref, shift in (
        (second_side_ref, second_early_ref, jnp.where(lon_even, 0, HALO)),
        (first_side_ref, first_early_ref, jnp.where(lon_even, HALO, 0)),
    ):
        for group, tile in enumerate(side_tiles(HALO, lambda plane: second_ref[plane], shift)):
            out_ref[group, pl.ds(0, EARLY), :] = early_ref[group, pl.ds(0, EARLY), :]
            out_ref[group, pl.ds(EARLY, HALO), :] = tile


def joiner(lat_ref):
    even = lat_ref[0] % 2 == 0

    def joined(one, own, two):
        return jnp.concatenate([jnp.where(even, two, one), own, jnp.where(even, one, two)], axis=0)

    return joined


def evolve(scratch, slabs, strips, plain_of, bottom, twist, finish):
    raw, state, lap, east_diff, north_diff, wet, count, flat, press, matrix = scratch

    def at(slab, comp=0):
        return (comp * slabs + slab) * PITCH + 8

    def get(ref, start, rows):
        return ref[pl.ds(start, rows), :]

    def put(ref, start, value):
        ref[pl.ds(start, value.shape[0]), :] = value

    matrix[...] = neighbours()
    if strips:
        bottom = bottom - jnp.where(lane_ids(EXT) >= 64, float(PAIRS), 0.0)
    put(flat, 8, bottom)
    put(flat, PITCH + 8, STEP_DT * twist)
    for slab in range(slabs):
        value = jnp.where(bottom > float(slab), 1.0, 0.0)
        put(wet, at(slab), value)
        around = (get(wet, at(slab) - 1, EXT) + get(wet, at(slab) + 1, EXT)) + beside(value)
        put(count, at(slab), around)
        for comp in range(COMPS):
            plain = plain_of(comp, slab)
            put(raw, at(slab, comp), plain)
            put(state, at(slab, comp), plain * value)

    a_windows = ((0, EXT), (0, EXT), (4, EXT - 8), (0, EXT))
    b_windows = ((0, EXT), (0, EXT), (4, EXT - 8), (HALO, ROWS))

    def before(step, batch):
        a_row, a_rows = a_windows[step]
        b_row, b_rows = b_windows[step]
        slope_of = raw if step == 0 else state
        fields = [(slab, comp) for slab in batch for comp in range(COMPS)]

        def lateral(ref):
            values = [in_two(get(ref, at(*field) + a_row, a_rows)) for field in fields]
            return jnp.dot(jnp.concatenate(values, axis=0), matrix[...], preferred_element_type=jnp.float32)

        both = lateral(state)
        slopes = lateral(raw) if step == 0 else both
        for index, (slab, comp) in enumerate(fields):
            w = get(wet, at(slab) + a_row, a_rows)
            n = get(count, at(slab) + a_row, a_rows)
            start = at(slab, comp)
            value = get(state, start + a_row, a_rows)
            along = get(state, start + a_row + 1, a_rows) + get(state, start + a_row - 1, a_rows)
            sums = both[index * a_rows : (index + 1) * a_rows, :LANES]
            put(lap, start + a_row, w * (along + sums - n * value))
            first = index * a_rows + b_row - a_row
            put(east_diff, start + b_row, slopes[first : first + b_rows, LANES:])
            put(north_diff, start + b_row, get(slope_of, start + b_row + 2, b_rows) - get(slope_of, start + b_row - 2, b_rows))

    scale = 0.5 * STEP_DT * GRAVITY

    def heavier(ref, slab, row, rows):
        return (scale * BETA_S) * get(ref, at(slab, 1) + row, rows) - (scale * ALPHA_T) * get(ref, at(slab, 0) + row, rows)

    def base(step):
        row, rows = b_windows[step]
        for slot, ref in enumerate((east_diff, north_diff)):
            total = None
            for slab in range(slabs):
                term = heavier(ref, slab, row, rows)
                total = term if total is None else total + term
            put(press, slot * PITCH + 8 + row, jnp.where(lane_ids(rows) >= 64, turned(64)(total), 0.0))

    def after(step, slab):
        row, rows = b_windows[step]
        w = get(wet, at(slab) + row, rows)
        n = get(count, at(slab) + row, rows)
        slopes = []
        for slot, ref in enumerate((east_diff, north_diff)):
            slope = heavier(ref, slab, row, rows)
            press_at = slot * PITCH + 8 + row
            if slab > 0 or strips:
                slope = slope + get(press, press_at, rows)
            put(press, press_at, slope)
            slopes.append(slope)
        twist_b = get(flat, PITCH + 8 + row, rows)
        bottom_b = get(flat, 8 + row, rows)
        keep = jnp.where(bottom_b == float(slab + 1), 1.0 - STEP_DT * DRAG_RATE, 1.0)
        old_zonal = get(state, at(slab, 2) + row, rows)
        old_merid = get(state, at(slab, 3) + row, rows)
        zonal = (-0.5 * STEP_DT) * old_zonal
        merid = (-0.5 * STEP_DT) * old_merid
        for comp in range(COMPS):
            start = at(slab, comp) + row
            value = get(lap, start, rows)
            along = get(lap, start + 1, rows) + get(lap, start - 1, rows)
            smooth = along + beside(value) - n * value
            new = zonal * get(east_diff, start, rows) + merid * get(north_diff, start, rows) - (STEP_DT * KAPPA) * smooth
            if comp < 2:
                new = new + get(state, start, rows)
            elif comp == 2:
                new = new + (keep * old_zonal + twist_b * old_merid - slopes[0])
            else:
                new = new + (keep * old_merid - twist_b * old_zonal - slopes[1])
            new = w * new
            if step < STEPS - 1:
                put(state, start, new)
            else:
                finish(comp, slab, new)

    batches = [tuple(range(first, min(first + BATCH, slabs))) for first in range(0, slabs, BATCH)]
    for batch in batches:
        before(0, batch)
    for step in range(STEPS):
        if strips:
            base(step)
        waiting = []
        for batch in batches:
            for slab in batch:
                after(step, slab)
            waiting.append(batch)
            if step < STEPS - 1 and len(waiting) > LAG:
                before(step + 1, waiting.pop(0))
        if step < STEPS - 1:
            for batch in waiting:
                before(step + 1, batch)


def block_kernel(lat_ref, fields_ref, flat_ref, second_ref, first_ref, out_ref, *scratch):
    read, joined = plane_reader(fields_ref, flat_ref), joiner(lat_ref)

    def ext(plane):
        return joined(first_ref[plane], read(plane, 0, ROWS), second_ref[plane])

    def finish(comp, slab, new):
        out_ref[comp, slab] = new

    evolve(
        scratch, LEVELS, False, lambda comp, slab: ext(comp * LEVELS + slab), ext(PLANES - 2), ext(PLANES - 1), finish
    )


def strips_kernel(
    lat_ref, lon_ref, fields_ref, flat_ref, second_ref, first_ref, sent_ref, early_ref, second_side_ref, first_side_ref, block_ref,
    out_any, out_ref, semaphores, *scratch, lat_count, lon_count,
):
    read, joined = plane_reader(fields_ref, flat_ref), joiner(lat_ref)
    lanes = lane_ids(EXT)
    upper = lanes >= 64
    place = lanes % 64
    lat, lon = lat_ref[0], lon_ref[0]
    lat_even, lon_even = lat % 2 == 0, lon % 2 == 0

    def ext(plane):
        return joined(first_ref[plane], read(plane, 0, ROWS), second_ref[plane])

    other = (jnp.where(lon_even, lon - 1, lon + 1) + lon_count) % lon_count
    seam = (lat == lat_count - 1) & (other == lon_count - 1 - lon)
    back = lane_ids(HALO) + 7 - 2 * (lane_ids(HALO) % 8)

    def in_order(value):
        early, late = value[:EARLY], value[EARLY:]
        return jnp.where(lat_even, jnp.concatenate([late, early], axis=0), jnp.concatenate([early, late], axis=0))

    from_west, from_east = [], []
    for group in range(GROUPS):
        index = 8 * group + lane_ids(HALO) % 64 // 8
        sign = jnp.where((index >= 2 * PAIRS) & (index < 4 * PAIRS), -1.0, 1.0)
        own = sign * folded(sent_ref[group, pl.ds(2 * HALO, HALO), :], back)
        at_seam = jnp.concatenate([early_ref[group, pl.ds(0, EARLY), :], own], axis=0)
        second = in_order(jnp.where(seam, at_seam, second_side_ref[group]))
        first = in_order(first_side_ref[group])
        from_west.append(jnp.where(lon_even, second, first))
        from_east.append(jnp.where(lon_even, first, second))

    def strip(index, low, high):
        group, slot = divmod(index, 8)
        value = jnp.where(upper, turned(64 + 8)(high), turned(8)(low))
        value = jnp.where((place >= 24) & (place < 40), jnp.where(upper, turned(64 + 40)(high), turned(40)(low)), value)
        value = jnp.where(place < 8, turned(-8 * slot)(from_west[group]), value)
        value = jnp.where((place >= 40) & (place < 48), turned(40 - 8 * slot)(from_east[group]), value)
        return value

    def plain_of(comp, slab):
        return strip(comp * PAIRS + slab, ext(comp * LEVELS + slab), ext(comp * LEVELS + slab + PAIRS))

    bottom, twist = ext(PLANES - 2), ext(PLANES - 1)
    own_lanes = lane_ids(ROWS)

    def leave(level):
        return pltpu.make_async_copy(out_ref.at[:, level], out_any.at[:, level], semaphores.at[level])

    def finish(comp, slab, new):
        for half in range(2):
            level = slab + half * PAIRS
            value = block_ref[comp, level]
            value = jnp.where(own_lanes < 8, turned(-8 - 64 * half)(new), value)
            out_ref[comp, level] = jnp.where(own_lanes >= 120, turned(120 - 32 - 64 * half)(new), value)
            if comp == COMPS - 1:
                leave(level).start()

    evolve(
        scratch, PAIRS, True, plain_of, strip(COMPS * PAIRS, bottom, bottom), strip(COMPS * PAIRS + 1, twist, twist), finish
    )
    for level in range(LEVELS):
        leave(level).wait()


def call(kernel, out_shape, scratch, flops, moved, *operands, out=pltpu.VMEM):
    places = [pltpu.SMEM if operand.shape == (1,) else pltpu.VMEM for operand in operands]
    return pl.pallas_call(
        kernel,
        out_shape=out_shape,
        in_specs=[pl.BlockSpec(memory_space=place) for place in places],
        out_specs=jax.tree.map(lambda _: pl.BlockSpec(memory_space=out), out_shape),
        scratch_shapes=scratch,
        compiler_params=pltpu.CompilerParams(vmem_limit_bytes=24 << 20),
        cost_estimate=pl.CostEstimate(flops=flops, bytes_accessed=moved, transcendentals=0),
    )(*operands)


def scratch_for(slabs):
    rows = lambda planes: pltpu.VMEM((planes * PITCH, LANES), jnp.float32)
    return (rows(COMPS * slabs),) * 5 + (rows(slabs),) * 2 + (rows(2),) * 2 + (pltpu.VMEM((2 * LANES, 2 * LANES), jnp.bfloat16),)


def local(fields, sea_mask, bottom_level, coriolis):
    del sea_mask
    lat_count, lon_count = lax.axis_size("lat"), lax.axis_size("lon")
    lat = lax.axis_index("lat").astype(jnp.int32).reshape(1)
    lon = lax.axis_index("lon").astype(jnp.int32).reshape(1)
    axes = ("lon", "lat")
    index_of = lambda lon, row: (lon % lon_count) * lat_count + row
    f32 = lambda *shape: jax.ShapeDtypeStruct(shape, jnp.float32)

    def other_side(i):
        return ((i + 1) ^ 1) - 1

    everywhere = [(i, j) for i in range(lon_count) for j in range(lat_count)]
    lat_first = [(index_of(i, j), index_of(i, j ^ 1)) for i, j in everywhere]
    lat_second = []
    for i, j in everywhere:
        if j == lat_count - 1:
            lat_second.append((index_of(i, j), index_of(lon_count - 1 - i, j)))
        elif j > 0:
            lat_second.append((index_of(i, j), index_of(i, other_side(j))))
    lon_first = [(index_of(i, j), index_of(i ^ 1, j)) for i, j in everywhere]
    lon_second = [(index_of(i, j), index_of(other_side(i), j)) for i, j in everywhere]
    at_seam = [j == lat_count - 1 and other_side(i) % lon_count == lon_count - 1 - i for i, j in everywhere]
    lon_early = [pair for pair, seam in zip(lon_second, at_seam, strict=True) if seam]
    lon_late = [pair for pair, seam in zip(lon_second, at_seam, strict=True) if not seam]

    flat = jnp.stack([bottom_level.astype(jnp.float32), coriolis])

    def half(value, dim, even):
        return jnp.where(
            even, lax.slice_in_dim(value, 0, HALO, axis=dim), lax.slice_in_dim(value, HALO, ROWS, axis=dim)
        )

    even = lat[0] % 2 == 0
    rows, even = lax.optimization_barrier((half(fields, 2, even), even))
    rows_message = f32(PLANES, HALO, LANES)
    to_second = jnp.concatenate([
        rows.reshape(COMPS * LEVELS, HALO, LANES),
        half(bottom_level, 0, even).astype(jnp.float32)[None],
        half(coriolis, 0, even)[None],
        jnp.zeros((1, HALO, LANES), jnp.float32),
    ])
    received = lax.ppermute(to_second, axes, lat_second)
    to_first = call(pack_first_kernel, rows_message, (), 10**5, 10**6, lat, fields, flat)
    first = lax.ppermute(to_first, axes, lat_first)
    to_second_early, to_first_early = call(
        pack_early_kernel, (f32(GROUPS, SPARE, LANES), f32(GROUPS, EARLY, LANES)), (), 10**5, 10**6,
        lat, lon, fields, flat, first,
    )
    early = lax.ppermute(to_second_early, axes, lon_early)
    second, to_second_side, to_first_side = call(
        functools.partial(pack_late_kernel, lat_count=lat_count), (rows_message,) + (f32(GROUPS, EXT, LANES),) * 2, (),
        10**5, 10**6, lat, lon, received, to_second_early, to_first_early,
    )
    second_side = lax.ppermute(to_second_side, axes, lon_late)
    first_side = lax.ppermute(to_first_side, axes, lon_first)
    result = f32(COMPS, LEVELS, ROWS, LANES)
    block = call(block_kernel, result, scratch_for(LEVELS), 10**9, 10**6, lat, fields, flat, second, first)
    return call(
        functools.partial(strips_kernel, lat_count=lat_count, lon_count=lon_count), result,
        (pltpu.VMEM(result.shape, jnp.float32), pltpu.SemaphoreType.DMA((LEVELS,))) + scratch_for(PAIRS), 10**8, 10**6,
        lat, lon, fields, flat, second, first, to_second_early, early, second_side, first_side, block, out=pltpu.HBM,
    )


def solution(mesh):
    in_specs = (P(None, None, "lat", "lon"), P(None, "lat", "lon"), P("lat", "lon"), P("lat", "lon"))
    out_specs = P(None, None, "lat", "lon")
    return jax.shard_map(local, mesh=mesh, in_specs=in_specs, out_specs=out_specs, check_vma=False)
```

```python
import functools

import jax
import jax.numpy as jnp
from jax import lax
from jax.experimental import pallas as pl
from jax.experimental.pallas import tpu as pltpu
from jax.sharding import PartitionSpec as P

STEPS = 4
STEP_DT = 0.1
KAPPA = 0.2
DRAG_RATE = 0.5
GRAVITY = 0.1
ALPHA_T = 0.2
BETA_S = 0.15

COMPS = 4
LEVELS = 10
PAIRS = LEVELS // 2
PLANES = COMPS * LEVELS + 2
ROWS = 16
HALO = 8
EXT = ROWS + 2 * HALO
EARLY = ROWS + HALO
SPARE = 48
PITCH = EXT + 16
LANES = 128
BATCH = 5
LAG = 1
GROUPS = 3


def lane_ids(rows):
    return lax.broadcasted_iota(jnp.int32, (rows, LANES), 1)


def turned(by):
    if by % LANES == 0:
        return lambda value: value
    return lambda value: pltpu.roll(value, by % LANES, 1)


def beside(value):
    return turned(-1)(value) + turned(1)(value)


def sloped(value):
    return turned(-2)(value) - turned(2)(value)


def in_two(value):
    high = value.astype(jnp.bfloat16)
    low = (value - high.astype(jnp.float32)).astype(jnp.bfloat16)
    return jnp.concatenate([high, low], axis=1)


def neighbours():
    source = lax.broadcasted_iota(jnp.int32, (2 * LANES, 2 * LANES), 0) % LANES
    target = lax.broadcasted_iota(jnp.int32, (2 * LANES, 2 * LANES), 1)
    east = (source - target) % LANES
    sums = jnp.where((east == 1) | (east == LANES - 1), 1.0, 0.0)
    slopes = jnp.where(east == 2, 1.0, jnp.where(east == LANES - 2, -1.0, 0.0))
    return jnp.where(target < LANES, sums, slopes).astype(jnp.bfloat16)


def pairs_of(plane_of):
    for index in range(COMPS * PAIRS + 2):
        comp, level = divmod(index, PAIRS)
        if comp < COMPS:
            low = plane_of(comp * LEVELS + level)
            yield index, low, plane_of(comp * LEVELS + level + PAIRS)
        else:
            value = plane_of(COMPS * LEVELS + index - COMPS * PAIRS)
            yield index, value, value


def plane_reader(fields_ref, flat_ref):
    def read(plane, start, rows):
        if plane >= COMPS * LEVELS:
            return flat_ref[plane - COMPS * LEVELS, pl.ds(start, rows), :]
        return fields_ref[plane // LEVELS, plane % LEVELS, pl.ds(start, rows), :]

    return read


def folded(value, lanes):
    rows = HALO - 1 - lax.broadcasted_iota(jnp.int32, (HALO, LANES), 0)
    return jnp.take_along_axis(jnp.take_along_axis(value, lanes, axis=1), rows, axis=0)


def pack_first_kernel(lat_ref, fields_ref, flat_ref, first_ref):
    read = plane_reader(fields_ref, flat_ref)
    row = pl.multiple_of(jnp.where(lat_ref[0] % 2 == 0, HALO, 0), HALO)
    for plane in range(PLANES):
        first_ref[plane] = read(plane, row, HALO)


def side_tiles(rows, plane_of, shift):
    lanes = lane_ids(rows)
    tiles = [jnp.zeros((rows, LANES), jnp.float32) for _ in range(GROUPS)]
    for index, low, high in pairs_of(plane_of):
        group, slot = divmod(index, 8)
        for at, value in ((8 * slot, low), (8 * slot + 64, high)):
            here = (lanes >= at) & (lanes < at + 8)
            tiles[group] = jnp.where(here, pltpu.roll(value, at + shift, 1), tiles[group])
    return tiles


def pack_own_kernel(lon_ref, fields_ref, flat_ref, second_own_ref, first_own_ref):
    read = plane_reader(fields_ref, flat_ref)
    lon_even = lon_ref[0] % 2 == 0
    for ref, shift in ((second_own_ref, jnp.where(lon_even, 0, HALO)), (first_own_ref, jnp.where(lon_even, HALO, 0))):
        for group, tile in enumerate(side_tiles(ROWS, lambda plane: read(plane, 0, ROWS), shift)):
            ref[group] = tile


def pack_early_kernel(lat_ref, lon_ref, first_ref, second_own_ref, first_own_ref, second_side_ref, first_side_ref):
    lat_even, lon_even = lat_ref[0] % 2 == 0, lon_ref[0] % 2 == 0
    own_at = pl.multiple_of(jnp.where(lat_even, 0, HALO), HALO)
    halo_at = pl.multiple_of(jnp.where(lat_even, ROWS, 0), HALO)
    for ref, own_ref, shift in (
        (second_side_ref, second_own_ref, jnp.where(lon_even, 0, HALO)),
        (first_side_ref, first_own_ref, jnp.where(lon_even, HALO, 0)),
    ):
        for group, tile in enumerate(side_tiles(HALO, lambda plane: first_ref[plane], shift)):
            ref[group, pl.ds(own_at, ROWS), :] = own_ref[group]
            ref[group, pl.ds(halo_at, HALO), :] = tile
    for group in range(GROUPS):
        for row in range(EARLY, SPARE, 8):
            second_side_ref[group, pl.ds(row, 8), :] = jnp.zeros((8, LANES), jnp.float32)


def pack_late_kernel(
    lat_ref, lon_ref, received_ref, second_early_ref, first_early_ref, second_ref, second_side_ref, first_side_ref, *, lat_count
):
    lat, lon_even = lat_ref[0], lon_ref[0] % 2 == 0

    @pl.when(lat < lat_count - 1)
    def _():
        for plane in range(PLANES):
            second_ref[plane] = received_ref[plane]

    @pl.when(lat == lat_count - 1)
    def _():
        back = LANES - 1 - lane_ids(HALO)
        for plane in range(PLANES):
            value = folded(received_ref[plane], back)
            second_ref[plane] = -value if 2 * LEVELS <= plane < 4 * LEVELS else value

    for out_ref, early_ref, shift in (
        (second_side_ref, second_early_ref, jnp.where(lon_even, 0, HALO)),
        (first_side_ref, first_early_ref, jnp.where(lon_even, HALO, 0)),
    ):
        for group, tile in enumerate(side_tiles(HALO, lambda plane: second_ref[plane], shift)):
            out_ref[group, pl.ds(0, EARLY), :] = early_ref[group, pl.ds(0, EARLY), :]
            out_ref[group, pl.ds(EARLY, HALO), :] = tile


def joiner(lat_ref):
    even = lat_ref[0] % 2 == 0

    def joined(one, own, two):
        return jnp.concatenate([jnp.where(even, two, one), own, jnp.where(even, one, two)], axis=0)

    return joined


def evolve(scratch, slabs, strips, plain_of, bottom, twist, finish):
    raw, state, lap, east_diff, north_diff, wet, count, flat, press, matrix = scratch

    def at(slab, comp=0):
        return (comp * slabs + slab) * PITCH + 8

    def get(ref, start, rows):
        return ref[pl.ds(start, rows), :]

    def put(ref, start, value):
        ref[pl.ds(start, value.shape[0]), :] = value

    matrix[...] = neighbours()
    if strips:
        bottom = bottom - jnp.where(lane_ids(EXT) >= 64, float(PAIRS), 0.0)
    put(flat, 8, bottom)
    put(flat, PITCH + 8, STEP_DT * twist)
    for slab in range(slabs):
        value = jnp.where(bottom > float(slab), 1.0, 0.0)
        put(wet, at(slab), value)
        around = (get(wet, at(slab) - 1, EXT) + get(wet, at(slab) + 1, EXT)) + beside(value)
        put(count, at(slab), around)
        for comp in range(COMPS):
            plain = plain_of(comp, slab)
            put(raw, at(slab, comp), plain)
            put(state, at(slab, comp), plain * value)

    a_windows = ((0, EXT), (0, EXT), (4, EXT - 8), (0, EXT))
    b_windows = ((0, EXT), (0, EXT), (4, EXT - 8), (HALO, ROWS))

    def before(step, batch):
        a_row, a_rows = a_windows[step]
        b_row, b_rows = b_windows[step]
        slope_of = raw if step == 0 else state
        fields = [(slab, comp) for slab in batch for comp in range(COMPS)]

        def lateral(ref):
            values = [in_two(get(ref, at(*field) + a_row, a_rows)) for field in fields]
            return jnp.dot(jnp.concatenate(values, axis=0), matrix[...], preferred_element_type=jnp.float32)

        both = lateral(state)
        slopes = lateral(raw) if step == 0 else both
        for index, (slab, comp) in enumerate(fields):
            w = get(wet, at(slab) + a_row, a_rows)
            n = get(count, at(slab) + a_row, a_rows)
            start = at(slab, comp)
            value = get(state, start + a_row, a_rows)
            along = get(state, start + a_row + 1, a_rows) + get(state, start + a_row - 1, a_rows)
            sums = both[index * a_rows : (index + 1) * a_rows, :LANES]
            put(lap, start + a_row, w * (along + sums - n * value))
            first = index * a_rows + b_row - a_row
            put(east_diff, start + b_row, slopes[first : first + b_rows, LANES:])
            put(north_diff, start + b_row, get(slope_of, start + b_row + 2, b_rows) - get(slope_of, start + b_row - 2, b_rows))

    scale = 0.5 * STEP_DT * GRAVITY

    def heavier(ref, slab, row, rows):
        return (scale * BETA_S) * get(ref, at(slab, 1) + row, rows) - (scale * ALPHA_T) * get(ref, at(slab, 0) + row, rows)

    def base(step):
        row, rows = b_windows[step]
        for slot, ref in enumerate((east_diff, north_diff)):
            total = None
            for slab in range(slabs):
                term = heavier(ref, slab, row, rows)
                total = term if total is None else total + term
            put(press, slot * PITCH + 8 + row, jnp.where(lane_ids(rows) >= 64, turned(64)(total), 0.0))

    def after(step, slab):
        row, rows = b_windows[step]
        w = get(wet, at(slab) + row, rows)
        n = get(count, at(slab) + row, rows)
        slopes = []
        for slot, ref in enumerate((east_diff, north_diff)):
            slope = heavier(ref, slab, row, rows)
            press_at = slot * PITCH + 8 + row
            if slab > 0 or strips:
                slope = slope + get(press, press_at, rows)
            put(press, press_at, slope)
            slopes.append(slope)
        twist_b = get(flat, PITCH + 8 + row, rows)
        bottom_b = get(flat, 8 + row, rows)
        keep = jnp.where(bottom_b == float(slab + 1), 1.0 - STEP_DT * DRAG_RATE, 1.0)
        old_zonal = get(state, at(slab, 2) + row, rows)
        old_merid = get(state, at(slab, 3) + row, rows)
        zonal = (-0.5 * STEP_DT) * old_zonal
        merid = (-0.5 * STEP_DT) * old_merid
        for comp in range(COMPS):
            start = at(slab, comp) + row
            value = get(lap, start, rows)
            along = get(lap, start + 1, rows) + get(lap, start - 1, rows)
            smooth = along + beside(value) - n * value
            new = zonal * get(east_diff, start, rows) + merid * get(north_diff, start, rows) - (STEP_DT * KAPPA) * smooth
            if comp < 2:
                new = new + get(state, start, rows)
            elif comp == 2:
                new = new + (keep * old_zonal + twist_b * old_merid - slopes[0])
            else:
                new = new + (keep * old_merid - twist_b * old_zonal - slopes[1])
            new = w * new
            if step < STEPS - 1:
                put(state, start, new)
            else:
                finish(comp, slab, new)

    batches = [tuple(range(first, min(first + BATCH, slabs))) for first in range(0, slabs, BATCH)]
    for batch in batches:
        before(0, batch)
    for step in range(STEPS):
        if strips:
            base(step)
        waiting = []
        for batch in batches:
            for slab in batch:
                after(step, slab)
            waiting.append(batch)
            if step < STEPS - 1 and len(waiting) > LAG:
                before(step + 1, waiting.pop(0))
        if step < STEPS - 1:
            for batch in waiting:
                before(step + 1, batch)


def block_kernel(lat_ref, fields_ref, flat_ref, second_ref, first_ref, out_ref, *scratch):
    read, joined = plane_reader(fields_ref, flat_ref), joiner(lat_ref)

    def ext(plane):
        return joined(first_ref[plane], read(plane, 0, ROWS), second_ref[plane])

    def finish(comp, slab, new):
        out_ref[comp, slab] = new

    evolve(
        scratch, LEVELS, False, lambda comp, slab: ext(comp * LEVELS + slab), ext(PLANES - 2), ext(PLANES - 1), finish
    )


def strips_kernel(
    lat_ref, lon_ref, fields_ref, flat_ref, second_ref, first_ref, sent_ref, early_ref, second_side_ref, first_side_ref, block_ref,
    out_any, out_ref, semaphores, *scratch, lat_count, lon_count,
):
    read, joined = plane_reader(fields_ref, flat_ref), joiner(lat_ref)
    lanes = lane_ids(EXT)
    upper = lanes >= 64
    place = lanes % 64
    lat, lon = lat_ref[0], lon_ref[0]
    lat_even, lon_even = lat % 2 == 0, lon % 2 == 0

    def ext(plane):
        return joined(first_ref[plane], read(plane, 0, ROWS), second_ref[plane])

    other = (jnp.where(lon_even, lon - 1, lon + 1) + lon_count) % lon_count
    seam = (lat == lat_count - 1) & (other == lon_count - 1 - lon)
    back = lane_ids(HALO) + 7 - 2 * (lane_ids(HALO) % 8)

    def in_order(value):
        early, late = value[:EARLY], value[EARLY:]
        return jnp.where(lat_even, jnp.concatenate([late, early], axis=0), jnp.concatenate([early, late], axis=0))

    from_west, from_east = [], []
    for group in range(GROUPS):
        index = 8 * group + lane_ids(HALO) % 64 // 8
        sign = jnp.where((index >= 2 * PAIRS) & (index < 4 * PAIRS), -1.0, 1.0)
        own = sign * folded(sent_ref[group, pl.ds(2 * HALO, HALO), :], back)
        at_seam = jnp.concatenate([early_ref[group, pl.ds(0, EARLY), :], own], axis=0)
        second = in_order(jnp.where(seam, at_seam, second_side_ref[group]))
        first = in_order(first_side_ref[group])
        from_west.append(jnp.where(lon_even, second, first))
        from_east.append(jnp.where(lon_even, first, second))

    def strip(index, low, high):
        group, slot = divmod(index, 8)
        value = jnp.where(upper, turned(64 + 8)(high), turned(8)(low))
        value = jnp.where((place >= 24) & (place < 40), jnp.where(upper, turned(64 + 40)(high), turned(40)(low)), value)
        value = jnp.where(place < 8, turned(-8 * slot)(from_west[group]), value)
        value = jnp.where((place >= 40) & (place < 48), turned(40 - 8 * slot)(from_east[group]), value)
        return value

    def plain_of(comp, slab):
        return strip(comp * PAIRS + slab, ext(comp * LEVELS + slab), ext(comp * LEVELS + slab + PAIRS))

    bottom, twist = ext(PLANES - 2), ext(PLANES - 1)
    own_lanes = lane_ids(ROWS)

    def leave(level):
        return pltpu.make_async_copy(out_ref.at[:, level], out_any.at[:, level], semaphores.at[level])

    def finish(comp, slab, new):
        for half in range(2):
            level = slab + half * PAIRS
            value = block_ref[comp, level]
            value = jnp.where(own_lanes < 8, turned(-8 - 64 * half)(new), value)
            out_ref[comp, level] = jnp.where(own_lanes >= 120, turned(120 - 32 - 64 * half)(new), value)
            if comp == COMPS - 1:
                leave(level).start()

    evolve(
        scratch, PAIRS, True, plain_of, strip(COMPS * PAIRS, bottom, bottom), strip(COMPS * PAIRS + 1, twist, twist), finish
    )
    for level in range(LEVELS):
        leave(level).wait()


def call(kernel, out_shape, scratch, flops, moved, *operands, out=pltpu.VMEM):
    places = [pltpu.SMEM if operand.shape == (1,) else pltpu.VMEM for operand in operands]
    return pl.pallas_call(
        kernel,
        out_shape=out_shape,
        in_specs=[pl.BlockSpec(memory_space=place) for place in places],
        out_specs=jax.tree.map(lambda _: pl.BlockSpec(memory_space=out), out_shape),
        scratch_shapes=scratch,
        compiler_params=pltpu.CompilerParams(vmem_limit_bytes=24 << 20),
        cost_estimate=pl.CostEstimate(flops=flops, bytes_accessed=moved, transcendentals=0),
    )(*operands)


def scratch_for(slabs):
    rows = lambda planes: pltpu.VMEM((planes * PITCH, LANES), jnp.float32)
    return (rows(COMPS * slabs),) * 5 + (rows(slabs),) * 2 + (rows(2),) * 2 + (pltpu.VMEM((2 * LANES, 2 * LANES), jnp.bfloat16),)


def local(fields, sea_mask, bottom_level, coriolis):
    del sea_mask
    lat_count, lon_count = lax.axis_size("lat"), lax.axis_size("lon")
    lat = lax.axis_index("lat").astype(jnp.int32).reshape(1)
    lon = lax.axis_index("lon").astype(jnp.int32).reshape(1)
    axes = ("lon", "lat")
    index_of = lambda lon, row: (lon % lon_count) * lat_count + row
    f32 = lambda *shape: jax.ShapeDtypeStruct(shape, jnp.float32)

    def other_side(i):
        return ((i + 1) ^ 1) - 1

    everywhere = [(i, j) for i in range(lon_count) for j in range(lat_count)]
    lat_first = [(index_of(i, j), index_of(i, j ^ 1)) for i, j in everywhere]
    lat_second = []
    for i, j in everywhere:
        if j == lat_count - 1:
            lat_second.append((index_of(i, j), index_of(lon_count - 1 - i, j)))
        elif j > 0:
            lat_second.append((index_of(i, j), index_of(i, other_side(j))))
    lon_first = [(index_of(i, j), index_of(i ^ 1, j)) for i, j in everywhere]
    lon_second = [(index_of(i, j), index_of(other_side(i), j)) for i, j in everywhere]
    at_seam = [j == lat_count - 1 and other_side(i) % lon_count == lon_count - 1 - i for i, j in everywhere]
    lon_early = [pair for pair, seam in zip(lon_second, at_seam, strict=True) if seam]
    lon_late = [pair for pair, seam in zip(lon_second, at_seam, strict=True) if not seam]

    flat = jnp.stack([bottom_level.astype(jnp.float32), coriolis])

    def half(value, dim, even):
        return jnp.where(
            even, lax.slice_in_dim(value, 0, HALO, axis=dim), lax.slice_in_dim(value, HALO, ROWS, axis=dim)
        )

    even = lat[0] % 2 == 0
    rows, even = lax.optimization_barrier((half(fields, 2, even), even))
    rows_message = f32(PLANES, HALO, LANES)
    to_second = jnp.concatenate([
        rows.reshape(COMPS * LEVELS, HALO, LANES),
        half(bottom_level, 0, even).astype(jnp.float32)[None],
        half(coriolis, 0, even)[None],
        jnp.zeros((1, HALO, LANES), jnp.float32),
    ])
    received = lax.ppermute(to_second, axes, lat_second)
    to_first = call(pack_first_kernel, rows_message, (), 10**5, 10**6, lat, fields, flat)
    first = lax.ppermute(to_first, axes, lat_first)
    second_own, first_own = call(pack_own_kernel, (f32(GROUPS, ROWS, LANES),) * 2, (), 10**5, 10**6, lon, fields, flat)
    to_second_early, to_first_early = call(
        pack_early_kernel, (f32(GROUPS, SPARE, LANES), f32(GROUPS, EARLY, LANES)), (), 10**5, 10**6,
        lat, lon, first, second_own, first_own,
    )
    early = lax.ppermute(to_second_early, axes, lon_early)
    second, to_second_side, to_first_side = call(
        functools.partial(pack_late_kernel, lat_count=lat_count), (rows_message,) + (f32(GROUPS, EXT, LANES),) * 2, (),
        10**5, 10**6, lat, lon, received, to_second_early, to_first_early,
    )
    second_side = lax.ppermute(to_second_side, axes, lon_late)
    first_side = lax.ppermute(to_first_side, axes, lon_first)
    result = f32(COMPS, LEVELS, ROWS, LANES)
    block = call(block_kernel, result, scratch_for(LEVELS), 10**9, 10**6, lat, fields, flat, second, first)
    return call(
        functools.partial(strips_kernel, lat_count=lat_count, lon_count=lon_count), result,
        (pltpu.VMEM(result.shape, jnp.float32), pltpu.SemaphoreType.DMA((LEVELS,))) + scratch_for(PAIRS), 10**8, 10**6,
        lat, lon, fields, flat, second, first, to_second_early, early, second_side, first_side, block, out=pltpu.HBM,
    )


def solution(mesh):
    in_specs = (P(None, None, "lat", "lon"), P(None, "lat", "lon"), P("lat", "lon"), P("lat", "lon"))
    out_specs = P(None, None, "lat", "lon")
    return jax.shard_map(local, mesh=mesh, in_specs=in_specs, out_specs=out_specs, check_vma=False)
```
